32 devices in a mesh: groups: 2 (over y), box: 8 (over z, x), trial: 2 (over core).
Axes of the slice: x: 2, y: 2, z: 4, core: 2. Of those that a mesh axis runs over, the one named last changes fastest.
Arguments:
- medium: float32 [4, 3, 8, 128, 128], P('trial', None, None, 'box'), may hold values from 0.5 to 2, as said below
- store: float32 [32, 3, 256], P(('groups', 'box', 'trial')), parts along dimension 0, may hold values from -6 to 6
- surf_off: int32 [256], replicated, may hold values from 0 to 16383, as said below
- owners: int32 [6], replicated, may hold values from 0 to 15, as said below
- brick_map: int32 [8], replicated, may hold values from 0 to 7, each once
Outputs:
- velocity: float32 [8, 3, 8, 128, 128], P(('groups', 'trial'), None, 'box'), parts along dimension 0
- stress: float32 [8, 6, 8, 128, 128], P(('groups', 'trial'), None, 'box'), parts along dimension 0
The draws below stay inside these ranges and needn't reach their ends.
There are 2 independent parts, one for each index of `groups`. The reference program is written for one: setup_inputs(seed, part) draws one part's arguments, and reference() takes and returns one part's arrays. A program takes and returns all parts, laid end to end along the dimension named above; an argument that names none is the same for every part. Nothing has to cross between parts.
Inputs may be any that keep to these rules, and one draw needn't show every extreme that they name: `surf_off`: entries k * 32 to (k+1) * 32 - 1 name distinct cells y * 128 + z of x-plane k. `owners`: distinct slots. `brick_map`: a permutation. `medium`: lam within 1 to 2, mu and buoyancy within 0.5 to 1.
All inputs are finite; a program needn't handle non-finite values.
Results may differ from the reference program's by a relative error of at most 0.00002.
Values sent between devices are 32-bit elements; how exact they have to be, the bound alone decides.
No kernel may reach another device: no remote copies, remote signals or barrier semaphores. Data moves between devices by JAX's collectives and lax.ppermute only.
A program may use at most 64 MiB of HBM per device.

```python
import jax
import jax.numpy as jnp
from jax import lax

NY = 128
NZ = 128
STEPS = 6
PER = 32
NX = 8
TRIALS = 4
BY = 16
SURF = 256
HOLDERS = 16
N_BOX = 8


def draw_surf_off(key, part):
    key = jax.random.fold_in(key, 11)
    cells = NY * NZ
    plane_keys = jax.random.split(key, NX)
    chosen = jax.vmap(lambda plane_key: jax.random.permutation(plane_key, cells - 2)[:PER])(plane_keys) + 1
    chosen = chosen.at[0, 0].set(0).at[NX - 1, 0].set(cells - 1)
    return chosen.reshape(SURF).astype(jnp.int32)


def draw_owners(key, part):
    key = jax.random.fold_in(key, 12)
    others = jax.random.permutation(jax.random.fold_in(key, 1), HOLDERS - 1)[:STEPS - 1]
    slot_at = jax.random.randint(jax.random.fold_in(key, 2), (), 0, STEPS)
    counter = jnp.arange(STEPS, dtype=jnp.int32)
    before = others[jnp.clip(counter, 0, STEPS - 2)]
    after = others[jnp.clip(counter - 1, 0, STEPS - 2)]
    chosen = jnp.where(counter < slot_at, before, jnp.where(counter == slot_at, HOLDERS - 1, after))
    return chosen.astype(jnp.int32)


def draw_medium(key, part):
    key = jax.random.fold_in(key, 13)
    shape = (TRIALS, 3, NX, NY, NZ)
    level = jax.random.uniform(jax.random.fold_in(key, 1), shape, jnp.float32)
    lowest = jnp.array([1.0, 0.5, 0.5], jnp.float32)[None, :, None, None, None]
    highest = jnp.array([2.0, 1.0, 1.0], jnp.float32)[None, :, None, None, None]
    return (lowest + (highest - lowest) * level).astype(jnp.float32)


def levels(stream_key, dims, shards, smallest, top_value):
    gain, own = 1.0, jax.random.fold_in(stream_key, 6)
    for position, blocks in shards:
        draws = jnp.exp(jax.random.uniform(jax.random.fold_in(own, position), (blocks,), jnp.float32, smallest / len(shards), top_value / len(shards)))
        gain = gain * jnp.repeat(draws, dims[position] // blocks).reshape([-1 if axis == position else 1 for axis in range(len(dims))])
    return gain


def scatter_about(stream_key, dims, deviation, reach, pieces=(), kind=jnp.bfloat16):
    result = jax.random.normal(stream_key, dims, jnp.float32) * deviation
    if len(pieces) > 0:
        result = levels(stream_key, dims, pieces, -0.22, 0.18) * result
    return jnp.clip(result, min=-reach, max=reach).astype(kind)


def setup_inputs(seed: int = 0, part: int = 0) -> dict:
    splits = jax.random.split(jax.random.key(seed), 6)
    part_keys = jax.random.split(jax.random.fold_in(splits[5], part), 6)
    return {
        "medium": draw_medium(jax.random.fold_in(splits[5], 71), part),
        "store": scatter_about(part_keys[1], (HOLDERS, 3, SURF), 1.0, 6.0, ((0, 16),), jnp.float32),
        "surf_off": draw_surf_off(jax.random.fold_in(splits[5], 71), part),
        "owners": draw_owners(jax.random.fold_in(splits[5], 71), part),
        "brick_map": jax.random.permutation(splits[4], N_BOX).astype(jnp.int32),
    }


TIME_STEP = 0.25


def forward(field, along):
    along = along % field.ndim
    widths = [(0, 0)] * field.ndim
    widths[along] = (0, 1)
    padded = jnp.pad(field, widths)
    return lax.slice_in_dim(padded, 1, field.shape[along] + 1, axis=along) - field


def backward(field, along):
    along = along % field.ndim
    widths = [(0, 0)] * field.ndim
    widths[along] = (1, 0)
    padded = jnp.pad(field, widths)
    return field - lax.slice_in_dim(padded, 0, field.shape[along], axis=along)


def reference(medium, store, surf_off, owners, brick_map):
    inverse = jnp.zeros((N_BOX,), jnp.int32).at[brick_map].set(jnp.arange(N_BOX, dtype=jnp.int32))
    blocks = medium.reshape(TRIALS, 3, NX, N_BOX, BY, NZ)
    physical = jnp.take(blocks, inverse, axis=3).reshape(TRIALS, 3, NX, NY, NZ)
    planes = jnp.broadcast_to(jnp.arange(NX, dtype=jnp.int32)[:, None], (NX, PER))
    offsets = surf_off.reshape(NX, PER)

    def injection(moment):
        surface_row = store[owners[moment]].reshape(3, NX, PER)
        spread = jnp.zeros((3, NX, NY * NZ), jnp.float32).at[:, planes, offsets].add(surface_row)
        return spread.reshape(3, NX, NY, NZ)

    def one_trial(medium_box):
        lame_first, shear_mod, buoyancy = medium_box[0], medium_box[1], medium_box[2]
        empty = jnp.zeros((NX, NY, NZ), jnp.float32)
        vel_x, vel_y, vel_z = empty, empty, empty
        sig_xx, sig_yy, sig_zz, sig_xy, sig_xz, sig_yz = empty, empty, empty, empty, empty, empty
        for moment in range(STEPS):
            injected = injection(moment)
            vel_x = vel_x + TIME_STEP * buoyancy * (forward(sig_xx, 0) + backward(sig_xy, 1) + backward(sig_xz, 2)) + injected[0]
            vel_y = vel_y + TIME_STEP * buoyancy * (backward(sig_xy, 0) + forward(sig_yy, 1) + backward(sig_yz, 2)) + injected[1]
            vel_z = vel_z + TIME_STEP * buoyancy * (backward(sig_xz, 0) + backward(sig_yz, 1) + forward(sig_zz, 2)) + injected[2]
            grad_xx = backward(vel_x, 0)
            grad_yy = backward(vel_y, 1)
            grad_zz = backward(vel_z, 2)
            divergence = grad_xx + grad_yy + grad_zz
            sig_xx = sig_xx + TIME_STEP * (lame_first * divergence + 2.0 * shear_mod * grad_xx)
            sig_yy = sig_yy + TIME_STEP * (lame_first * divergence + 2.0 * shear_mod * grad_yy)
            sig_zz = sig_zz + TIME_STEP * (lame_first * divergence + 2.0 * shear_mod * grad_zz)
            sig_xy = sig_xy + TIME_STEP * shear_mod * (forward(vel_x, 1) + forward(vel_y, 0))
            sig_xz = sig_xz + TIME_STEP * shear_mod * (forward(vel_x, 2) + forward(vel_z, 0))
            sig_yz = sig_yz + TIME_STEP * shear_mod * (forward(vel_y, 2) + forward(vel_z, 1))
        return (jnp.stack([vel_x, vel_y, vel_z]),
                jnp.stack([sig_xx, sig_yy, sig_zz, sig_xy, sig_xz, sig_yz]))

    velocity, stress = lax.map(one_trial, physical)
    return velocity, stress
```

```python
import functools

import jax
import jax.numpy as jnp
from jax import lax
from jax.experimental import pallas as pl
from jax.experimental.pallas import tpu as pltpu
from jax.sharding import PartitionSpec as P

STEPS = 6
TIME_STEP = 0.25
VX, VY, VZ, XX, YY, ZZ, XY, XZ, YZ = range(9)
PAD = 8
ROWS = 8


def propagate(bricks, geo_ref, med_ref, vals_ref, offs_ref, vel_ref, str_ref, fields, pieces, hot_y, hot_z):
    trials = med_ref.shape[1]
    planes = med_ref.shape[3]
    block_y = med_ref.shape[4]
    cells_y, cells_z = vel_ref.shape[3], vel_ref.shape[4]
    per = vals_ref.shape[2] // 4
    chunks = cells_y // ROWS
    centre = geo_ref[0]
    lane = lax.broadcasted_iota(jnp.int32, (ROWS, cells_z), 1)
    first_lane = lane == 0
    last_lane = lane == cells_z - 1

    def back_z(value):
        return value - jnp.where(first_lane, 0.0, pltpu.roll(value, 1, 1))

    def fore_z(value):
        return jnp.where(last_lane, 0.0, pltpu.roll(value, cells_z - 1, 1)) - value

    side = jnp.zeros((PAD, cells_z), jnp.float32)
    for field in (XY, YZ, VY):
        for plane in range(planes):
            fields[field, plane + 1, 0:PAD, :] = side
    for field in (YY, VX, VZ):
        for plane in range(planes):
            fields[field, plane + 1, PAD + cells_y : PAD + cells_y + PAD, :] = side
    outside = jnp.zeros((cells_y, cells_z), jnp.float32)
    for field in (XY, XZ, VX):
        fields[field, 0, PAD : PAD + cells_y, :] = outside
    for field in (XX, VY, VZ):
        fields[field, planes + 1, PAD : PAD + cells_y, :] = outside

    kept = lax.broadcasted_iota(jnp.int32, vals_ref.shape, 2)
    value = vals_ref[...]
    high = value.astype(jnp.bfloat16).astype(jnp.float32)
    rest = value - high
    middle = rest.astype(jnp.bfloat16).astype(jnp.float32)
    low = rest - middle
    pieces[...] = jnp.where(
        kept < per, high, jnp.where(kept < 2 * per, middle, jnp.where(kept < 3 * per, low, 0.0))
    )
    row_id = lax.broadcasted_iota(jnp.int32, (cells_y, offs_ref.shape[1]), 0)
    column_id = lax.broadcasted_iota(jnp.int32, (cells_z, offs_ref.shape[1]), 0)
    for plane in range(planes):
        offsets = offs_ref[plane : plane + 1, :]
        hot_y[plane] = jnp.where(row_id == offsets // cells_z, 1.0, 0.0).astype(jnp.bfloat16)
        hot_z[plane] = jnp.where(column_id == offsets % cells_z, 1.0, 0.0)

    def injection(step, comp, plane):
        row = pieces[step * 3 + comp, pl.ds(plane, 1), :]
        return lax.dot_general(
            hot_y[plane],
            (hot_z[plane] * row).astype(jnp.bfloat16),
            (((1,), (1,)), ((), ())),
            preferred_element_type=jnp.float32,
        )

    def limits(step):
        reach = STEPS - 1 - step
        return jnp.maximum(centre - reach, 0), jnp.minimum(centre + reach, planes - 1)

    def one_trial(trial, carry):
        def medium(component, plane, chunk):
            row = chunk * ROWS
            return med_ref[
                geo_ref[1 + row // block_y], trial, component, plane,
                row % block_y : row % block_y + ROWS, :
            ]

        def at(field, plane, chunk, shift=0):
            row = PAD + chunk * ROWS + shift
            return fields[field, plane + 1, row : row + ROWS, :]

        def put(field, plane, chunk, value):
            row = PAD + chunk * ROWS
            fields[field, plane + 1, row : row + ROWS, :] = value

        def start_velocity(plane, carry):
            for comp in range(3):
                fields[comp, plane + 1, PAD : PAD + cells_y, :] = injection(0, comp, plane)
            return carry

        def velocity_x(step, plane, carry):
            added = injection(step, 0, plane)
            for chunk in range(chunks):
                xx, xy, xz = (at(f, plane, chunk) for f in (XX, XY, XZ))
                pull = (at(XX, plane + 1, chunk) - xx) + (xy - at(XY, plane, chunk, -1)) + back_z(xz)
                gain = TIME_STEP * medium(2, plane, chunk)
                new = at(VX, plane, chunk) + gain * pull + added[chunk * ROWS : chunk * ROWS + ROWS]
                put(VX, plane, chunk, new)
            return carry

        def velocity_yz(step, plane, carry):
            added_y = injection(step, 1, plane)
            added_z = injection(step, 2, plane)
            for chunk in range(chunks):
                here = slice(chunk * ROWS, chunk * ROWS + ROWS)
                gain = TIME_STEP * medium(2, plane, chunk)
                yz = at(YZ, plane, chunk)
                pull = (
                    (at(XY, plane, chunk) - at(XY, plane - 1, chunk))
                    + (at(YY, plane, chunk, 1) - at(YY, plane, chunk))
                    + back_z(yz)
                )
                put(VY, plane, chunk, at(VY, plane, chunk) + gain * pull + added_y[here])
                pull = (
                    (at(XZ, plane, chunk) - at(XZ, plane - 1, chunk))
                    + (yz - at(YZ, plane, chunk, -1))
                    + fore_z(at(ZZ, plane, chunk))
                )
                put(VZ, plane, chunk, at(VZ, plane, chunk) + gain * pull + added_z[here])
            return carry

        def stress(first, plane, carry):
            for chunk in range(chunks):
                vx, vy, vz = (at(f, plane, chunk) for f in (VX, VY, VZ))
                lam = TIME_STEP * medium(0, plane, chunk)
                mu = TIME_STEP * medium(1, plane, chunk)
                twice = mu + mu
                grad_x = vx - at(VX, plane - 1, chunk)
                grad_y = vy - at(VY, plane, chunk, -1)
                grad_z = back_z(vz)
                spread = lam * (grad_x + grad_y + grad_z)
                changes = (
                    (XX, spread + twice * grad_x),
                    (YY, spread + twice * grad_y),
                    (ZZ, spread + twice * grad_z),
                    (XY, mu * ((at(VX, plane, chunk, 1) - vx) + (at(VY, plane + 1, chunk) - vy))),
                    (XZ, mu * (fore_z(vx) + (at(VZ, plane + 1, chunk) - vz))),
                    (YZ, mu * (fore_z(vy) + (at(VZ, plane, chunk, 1) - vz))),
                )
                for field, change in changes:
                    put(field, plane, chunk, change if first else at(field, plane, chunk) + change)
            return carry

        low, high = limits(0)
        lax.fori_loop(jnp.maximum(low - 1, 0), jnp.minimum(high + 2, planes), start_velocity, 0)
        lax.fori_loop(low, high + 1, functools.partial(stress, True), 0)

        def one_step(step, carry):
            low, high = limits(step)
            lax.fori_loop(jnp.maximum(low - 1, 0), high + 1, functools.partial(velocity_x, step), 0)
            lax.fori_loop(low, jnp.minimum(high + 2, planes), functools.partial(velocity_yz, step), 0)
            lax.fori_loop(low, high + 1, functools.partial(stress, False), 0)
            return carry

        lax.fori_loop(1, STEPS, one_step, 0)
        for field in range(3):
            vel_ref[trial, field, 0] = fields[field, centre + 1, PAD : PAD + cells_y, :]
        for field in range(6):
            str_ref[trial, field, 0] = fields[3 + field, centre + 1, PAD : PAD + cells_y, :]
        return carry

    lax.fori_loop(0, trials, one_trial, 0)


def run_steps(geometry, medium, values, offsets, cells_y, cells_z):
    bricks, trials, _, planes = medium.shape[:4]
    lanes = offsets.shape[1]
    return pl.pallas_call(
        functools.partial(propagate, bricks),
        out_shape=(
            jax.ShapeDtypeStruct((trials, 3, 1, cells_y, cells_z), jnp.float32),
            jax.ShapeDtypeStruct((trials, 6, 1, cells_y, cells_z), jnp.float32),
        ),
        in_specs=[pl.BlockSpec(memory_space=pltpu.SMEM)] + [pl.BlockSpec(memory_space=pltpu.VMEM)] * 3,
        out_specs=[pl.BlockSpec(memory_space=pltpu.VMEM)] * 2,
        scratch_shapes=[
            pltpu.VMEM((9, planes + 2, cells_y + 2 * PAD, cells_z), jnp.float32),
            pltpu.VMEM((3 * STEPS, planes, lanes), jnp.float32),
            pltpu.VMEM((planes, cells_y, lanes), jnp.bfloat16),
            pltpu.VMEM((planes, cells_z, lanes), jnp.float32),
        ],
        compiler_params=pltpu.CompilerParams(vmem_limit_bytes=48 * 1024 * 1024),
        cost_estimate=pl.CostEstimate(flops=30_000_000, bytes_accessed=5_000_000, transcendentals=0),
    )(geometry, medium, values, offsets)


def from_behind(value, axis, steps):
    count = lax.axis_size(axis)
    leading, last = (max(0, -steps), min(count, count - steps))
    return lax.ppermute(value, axis, [(source, source + steps) for source in range(leading, last)])


def per_device(medium, store, surf_off, owners, brick_map):
    boxes = lax.axis_size("box")
    place = lax.axis_index("box")
    trials_here, _, all_planes, brick_y, cells_z = medium.shape
    cells_y = boxes * brick_y
    per = surf_off.shape[0] // all_planes
    inverse = jnp.zeros((boxes,), jnp.int32).at[brick_map].set(jnp.arange(boxes, dtype=jnp.int32))
    offsets = surf_off.reshape(all_planes, per)
    reach = STEPS
    if all_planes <= 2 * reach + 1:
        window = lax.all_gather(medium, "box")
        rows = lax.all_gather(store[0], ("box", "trial"))[owners].reshape(STEPS * 3, all_planes, per)
        geometry = jnp.concatenate([place[None], inverse])
    else:
        moved = lax.all_to_all(medium, "box", split_axis=2, concat_axis=3, tiled=True)
        blocks = moved.reshape(trials_here, 3, 1, boxes, brick_y, cells_z)
        mine = jnp.take(blocks, inverse, axis=3).reshape(trials_here, 3, 1, cells_y, cells_z)
        window = jnp.concatenate(
            [from_behind(mine, "box", -shift) for shift in range(-reach, reach + 1)], axis=2
        )[None]
        slot = place * lax.axis_size("trial") + lax.axis_index("trial")
        rows = lax.psum(jnp.where((owners == slot)[:, None, None], store, 0.0), ("box", "trial"))
        rows = rows.reshape(STEPS * 3, all_planes, per)
        rows = jnp.pad(rows, ((0, 0), (reach, reach), (0, 0)))
        rows = lax.dynamic_slice_in_dim(rows, place, 2 * reach + 1, 1)
        offsets = jnp.pad(offsets, ((reach, reach), (0, 0)), constant_values=-1)
        offsets = lax.dynamic_slice_in_dim(offsets, place, 2 * reach + 1, 0)
        geometry = jnp.array([reach, 0], jnp.int32)
    values = jnp.tile(rows, (1, 1, 4))
    offsets = jnp.tile(offsets, (1, 4))
    return run_steps(geometry, window, values, offsets, cells_y, cells_z)


def solution(mesh):
    return jax.shard_map(
        per_device,
        mesh=mesh,
        in_specs=(
            P("trial", None, None, "box", None),
            P(("groups", "box", "trial"), None, None),
            P(),
            P(),
            P(),
        ),
        out_specs=(
            P(("groups", "trial"), None, "box", None, None),
            P(("groups", "trial"), None, "box", None, None),
        ),
        check_vma=False,
    )
```

```python
import functools

import jax
import jax.numpy as jnp
from jax import lax
from jax.experimental import pallas as pl
from jax.experimental.pallas import tpu as pltpu
from jax.sharding import PartitionSpec as P

STEPS = 6
TIME_STEP = 0.25
VX, VY, VZ, XX, YY, ZZ, XY, XZ, YZ = range(9)
ROWS = 8
LINES = 24


def ring_place(box, count):
    return jnp.where(box % 2 == 0, box // 2, count - 1 - box // 2)


def ring_box(place, count):
    return jnp.where(place < count // 2, 2 * place, 2 * (count - 1 - place) + 1)


def ring_offsets(count):
    steps = [0]
    for distance in range(1, count // 2):
        steps += [-distance, distance]
    return steps + [count // 2]


def split_values(value, per):
    group = lax.broadcasted_iota(jnp.int32, value.shape, 1) // per
    high = value.astype(jnp.bfloat16).astype(jnp.float32)
    rest = value - high
    middle = rest.astype(jnp.bfloat16).astype(jnp.float32)
    low = rest - middle
    return jnp.where(
        group == 0, high, jnp.where(group == 1, middle, jnp.where(group == 2, low, 0.0))
    )


class Plane:
    def __init__(self, fields, cells_y, cells_z):
        self.fields, self.chunks = fields, cells_y // ROWS
        row = lax.broadcasted_iota(jnp.int32, (ROWS, cells_z), 0)
        lane = lax.broadcasted_iota(jnp.int32, (ROWS, cells_z), 1)
        self.first_row, self.last_row = row == 0, row == ROWS - 1
        self.first_lane, self.last_lane = lane == 0, lane == cells_z - 1
        self.cells_z = cells_z
        self.loaded, self.rolled = {}, {}

    def at(self, field, plane, chunk, key):
        if (field, key, chunk) not in self.loaded:
            self.loaded[field, key, chunk] = self.fields[
                field, plane, chunk * ROWS : chunk * ROWS + ROWS, :
            ]
        return self.loaded[field, key, chunk]

    def roll_rows(self, field, plane, chunk, by):
        if not 0 <= chunk < self.chunks:
            return 0.0
        if (field, chunk) not in self.rolled:
            self.rolled[field, chunk] = pltpu.roll(self.at(field, plane, chunk, 0), by, 0)
        return self.rolled[field, chunk]

    def back_y(self, field, plane, chunk):
        here = self.roll_rows(field, plane, chunk, 1)
        before = self.roll_rows(field, plane, chunk - 1, 1)
        return self.at(field, plane, chunk, 0) - jnp.where(self.first_row, before, here)

    def fore_y(self, field, plane, chunk):
        here = self.roll_rows(field, plane, chunk, ROWS - 1)
        after = self.roll_rows(field, plane, chunk + 1, ROWS - 1)
        return jnp.where(self.last_row, after, here) - self.at(field, plane, chunk, 0)

    def back_z(self, value):
        return value - jnp.where(self.first_lane, 0.0, pltpu.roll(value, 1, 1))

    def fore_z(self, value):
        return jnp.where(self.last_lane, 0.0, pltpu.roll(value, self.cells_z - 1, 1)) - value


def propagate(plan, *refs):
    trial, count, planes, cells_y, cells_z, per, first = plan
    refs = list(refs)
    place_ref, map_ref, owners_ref = refs[:3]
    piece_refs = refs[3 : 3 + count]
    rest = refs[3 + count :]
    if count > 1 and first:
        hot_y, hot_z = rest[:2]
        rest = rest[2:]
    else:
        hot_y, hot_z, given_ref = rest[:3]
        rest = rest[3:]
    if not first:
        rest = rest[2:]
    vel_ref, str_ref = rest[:2]
    rest = rest[2:]
    if first:
        values = rest[0]
        rest = rest[1:]
    else:
        values = given_ref
    fields, medium, added, stored, lines, sems = rest
    block_y = cells_y // count
    chunks = cells_y // ROWS

    if count > 1:
        centre = place_ref[0]
        start = ring_place(centre, count)
        boxes = [ring_box(lax.rem(start + step + count, count), count) for step in ring_offsets(count)]
        blocks = [map_ref[box] for box in boxes]
    else:
        centre = planes // 2
        blocks = [0]
    for block, piece in zip(blocks, piece_refs):
        top = pl.multiple_of(block * block_y, 8)
        for component in range(3):
            for plane in range(planes):
                source = (component * planes + plane) * block_y
                medium[component, plane, pl.ds(top, block_y), :] = (
                    TIME_STEP * piece[source : source + block_y, :]
                )

    outside = jnp.zeros((cells_y, cells_z), jnp.float32)
    for field in (XY, XZ, VX):
        fields[field, 0] = outside
    for field in (XX, VY, VZ):
        fields[field, planes + 1] = outside

    if first and count > 1:
        halves = planes * per // cells_z
        for box, piece in zip(boxes, piece_refs):
            source = 3 * planes * block_y
            stored[box] = piece[source : source + 6 * halves + (-6 * halves) % ROWS, :]
        for step in range(STEPS):
            owner = owners_ref[step]
            for comp in range(3):
                for half in range(halves):
                    source = (owner % 2) * 3 * halves + comp * halves + half
                    lines[half, pl.ds(step * 3 + comp, 1), :] = stored[owner // 2, pl.ds(source, 1), :]
        for plane in range(planes):
            half, place = divmod(plane * per, cells_z)
            line = lines[half]
            group = lax.broadcasted_iota(jnp.int32, line.shape, 1) // per
            spread = pltpu.roll(line, (cells_z - place) % cells_z, 1) if place else line
            spread = jnp.where(
                group == 0,
                spread,
                jnp.where(group == 1, pltpu.roll(spread, per, 1), pltpu.roll(spread, 2 * per, 1)),
            )
            values[plane] = split_values(spread, per)
    elif first:
        for plane in range(planes):
            values[plane] = split_values(given_ref[plane], per)

    def injection(step, comp, plane):
        row = values[plane, pl.ds(step * 3 + comp, 1), :]
        return lax.dot_general(
            hot_y[plane],
            (hot_z[plane] * row).astype(jnp.bfloat16),
            (((1,), (1,)), ((), ())),
            preferred_element_type=jnp.float32,
        )

    def limits(step):
        reach = STEPS - 1 - step
        return jnp.maximum(centre - reach, 0), jnp.minimum(centre + reach, planes - 1)

    def medium_at(component, plane, chunk):
        return medium[component, plane, chunk * ROWS : chunk * ROWS + ROWS, :]

    def put(field, plane, chunk, value):
        fields[field, plane + 1, chunk * ROWS : chunk * ROWS + ROWS, :] = value

    def added_at(comp, plane, chunk):
        return added[comp, plane, chunk * ROWS : chunk * ROWS + ROWS, :]

    def start_velocity(plane, carry):
        for comp in range(3):
            fields[comp, plane + 1] = injection(0, comp, plane)
        return carry

    def velocity_x(plane, carry):
        here = Plane(fields, cells_y, cells_z)
        index = plane + 1
        for chunk in range(chunks):
            pull = (
                (here.at(XX, index + 1, chunk, 1) - here.at(XX, index, chunk, 0))
                + here.back_y(XY, index, chunk)
                + here.back_z(here.at(XZ, index, chunk, 0))
            )
            new = here.at(VX, index, chunk, 0) + medium_at(2, plane, chunk) * pull
            put(VX, plane, chunk, new + added_at(0, plane, chunk))
        return carry

    def velocity_yz(plane, carry):
        here = Plane(fields, cells_y, cells_z)
        index = plane + 1
        for chunk in range(chunks):
            gain = medium_at(2, plane, chunk)
            pull = (
                (here.at(XY, index, chunk, 0) - here.at(XY, index - 1, chunk, -1))
                + here.fore_y(YY, index, chunk)
                + here.back_z(here.at(YZ, index, chunk, 0))
            )
            new = here.at(VY, index, chunk, 0) + gain * pull
            put(VY, plane, chunk, new + added_at(1, plane, chunk))
            pull = (
                (here.at(XZ, index, chunk, 0) - here.at(XZ, index - 1, chunk, -1))
                + here.back_y(YZ, index, chunk)
                + here.fore_z(here.at(ZZ, index, chunk, 0))
            )
            new = here.at(VZ, index, chunk, 0) + gain * pull
            put(VZ, plane, chunk, new + added_at(2, plane, chunk))
        return carry

    def stress(step, fresh, final, plane, carry):
        here = Plane(fields, cells_y, cells_z)
        index = plane + 1
        if not final:
            for comp in range(3):
                added[comp, plane] = injection(step + 1, comp, plane)
        for chunk in range(chunks):
            vx, vy, vz = (here.at(field, index, chunk, 0) for field in (VX, VY, VZ))
            lam, mu = medium_at(0, plane, chunk), medium_at(1, plane, chunk)
            twice = mu + mu
            grad_x = vx - here.at(VX, index - 1, chunk, -1)
            grad_y = here.back_y(VY, index, chunk)
            grad_z = here.back_z(vz)
            spread = lam * (grad_x + grad_y + grad_z)
            changes = (
                (XX, spread + twice * grad_x),
                (YY, spread + twice * grad_y),
                (ZZ, spread + twice * grad_z),
                (XY, mu * (here.fore_y(VX, index, chunk) + (here.at(VY, index + 1, chunk, 1) - vy))),
                (XZ, mu * (here.fore_z(vx) + (here.at(VZ, index + 1, chunk, 1) - vz))),
                (YZ, mu * (here.fore_z(vy) + here.fore_y(VZ, index, chunk))),
            )
            for field, change in changes:
                put(field, plane, chunk, change if fresh else here.at(field, index, chunk, 0) + change)
        return carry

    def velocities(step):
        low, high = limits(step)
        lax.fori_loop(jnp.maximum(low - 1, 0), high + 1, velocity_x, 0)
        lax.fori_loop(low, jnp.minimum(high + 2, planes), velocity_yz, 0)

    low, high = limits(0)
    lax.fori_loop(jnp.maximum(low - 1, 0), jnp.minimum(high + 2, planes), start_velocity, 0)
    lax.fori_loop(low, high + 1, functools.partial(stress, 0, True, False), 0)

    def one_step(step, carry):
        velocities(step)
        low, high = limits(step)
        lax.fori_loop(low, high + 1, functools.partial(stress, step, False, False), 0)
        return carry

    lax.fori_loop(1, STEPS - 1, one_step, 0)
    velocities(STEPS - 1)
    stress(STEPS - 1, False, True, centre, 0)

    copies = (
        pltpu.make_async_copy(fields.at[0:3, centre + 1], vel_ref.at[trial, :, 0], sems.at[0]),
        pltpu.make_async_copy(fields.at[3:9, centre + 1], str_ref.at[trial, :, 0], sems.at[1]),
    )
    for copy in copies:
        copy.start()
    for copy in copies:
        copy.wait()


def run_trial(trial, trials, shape, scalars, pieces, hots, given, before):
    planes, cells_y, cells_z, per = shape
    count, first = len(pieces), before is None
    smem, vmem, anywhere = (
        pl.BlockSpec(memory_space=space) for space in (pltpu.SMEM, pltpu.VMEM, pl.ANY)
    )
    operands = list(scalars) + list(pieces) + list(hots)
    specs = [smem] * 3 + [vmem] * (len(operands) - 3)
    if given is not None:
        operands.append(given)
        specs.append(vmem)
    out_shape = [
        jax.ShapeDtypeStruct((trials, 3, 1, cells_y, cells_z), jnp.float32),
        jax.ShapeDtypeStruct((trials, 6, 1, cells_y, cells_z), jnp.float32),
    ]
    out_specs = [anywhere, anywhere]
    aliases = {}
    if first:
        out_shape.append(jax.ShapeDtypeStruct((planes, LINES, cells_z), jnp.float32))
        out_specs.append(vmem)
    else:
        aliases = {len(operands): 0, len(operands) + 1: 1}
        operands += list(before)
        specs += [anywhere, anywhere]
    return pl.pallas_call(
        functools.partial(propagate, (trial, count, planes, cells_y, cells_z, per, first)),
        out_shape=out_shape,
        in_specs=specs,
        out_specs=out_specs,
        input_output_aliases=aliases,
        scratch_shapes=[
            pltpu.VMEM((9, planes + 2, cells_y, cells_z), jnp.float32),
            pltpu.VMEM((3, planes, cells_y, cells_z), jnp.float32),
            pltpu.VMEM((3, planes, cells_y, cells_z), jnp.float32),
            pltpu.VMEM((count, 2 * ROWS, cells_z), jnp.float32),
            pltpu.VMEM((2, LINES, cells_z), jnp.float32),
            pltpu.SemaphoreType.DMA((2,)),
        ],
        compiler_params=pltpu.CompilerParams(vmem_limit_bytes=40 * 1024 * 1024),
        cost_estimate=pl.CostEstimate(flops=30_000_000, bytes_accessed=5_000_000, transcendentals=0),
    )(*operands)


def from_behind(value, axis, steps):
    count = lax.axis_size(axis)
    leading, last = (max(0, -steps), min(count, count - steps))
    return lax.ppermute(value, axis, [(source, source + steps) for source in range(leading, last)])


def around(medium, store, count):
    trials = medium.shape[0]
    lanes = medium.shape[-1]
    order = [2 * place for place in range((count + 1) // 2)]
    order += [box for box in range(count - 1, 0, -1) if box % 2 == 1]
    up = [(order[place], order[(place + 1) % count]) for place in range(count)]
    down = [(target, source) for source, target in up]
    mine = store[0].reshape(-1, lanes)
    other = lax.ppermute(mine, "trial", [(0, 1), (1, 0)])
    lower = lax.axis_index("trial") == 0
    rows = [jnp.where(lower, mine, other), jnp.where(lower, other, mine)]
    filler = jnp.zeros(((-2 * mine.shape[0]) % ROWS, lanes), jnp.float32)
    own = [medium[trial].reshape(-1, lanes) for trial in range(trials)]
    own[0] = jnp.concatenate([own[0]] + rows + [filler])
    pieces = [[piece] for piece in own]
    forth, back = list(own), list(own)
    for _ in range(1, count // 2):
        for trial in range(trials):
            forth[trial] = lax.ppermute(forth[trial], "box", up)
            back[trial] = lax.ppermute(back[trial], "box", down)
            pieces[trial] += [forth[trial], back[trial]]
    for trial in range(trials):
        if trial % 2 == 0:
            pieces[trial].append(lax.ppermute(forth[trial], "box", up))
        else:
            pieces[trial].append(lax.ppermute(back[trial], "box", down))
    return pieces


def hot_planes(offsets, cells_y, cells_z):
    rows = jnp.arange(cells_y, dtype=jnp.int32)[None, :, None]
    columns = jnp.arange(cells_z, dtype=jnp.int32)[None, :, None]
    hot_y = (offsets[:, None, :] // cells_z == rows).astype(jnp.bfloat16)
    hot_z = (offsets[:, None, :] % cells_z == columns).astype(jnp.float32)
    return hot_y, hot_z


def per_device(medium, store, surf_off, owners, brick_map):
    boxes = lax.axis_size("box")
    place = lax.axis_index("box")
    trials_here, _, all_planes, brick_y, cells_z = medium.shape
    cells_y = boxes * brick_y
    per = surf_off.shape[0] // all_planes
    offsets = surf_off.reshape(all_planes, per)
    reach = STEPS
    if all_planes <= 2 * reach + 1 and boxes == 8 and lax.axis_size("trial") == 2:
        pieces = around(medium, store, boxes)
        planes = all_planes
        given = None
        scalars = (place[None], brick_map, owners)
    else:
        inverse = jnp.zeros((boxes,), jnp.int32).at[brick_map].set(jnp.arange(boxes, dtype=jnp.int32))
        moved = lax.all_to_all(medium, "box", split_axis=2, concat_axis=3, tiled=True)
        blocks = moved.reshape(trials_here, 3, 1, boxes, brick_y, cells_z)
        mine = jnp.take(blocks, inverse, axis=3).reshape(trials_here, 3, 1, cells_y, cells_z)
        window = jnp.concatenate(
            [from_behind(mine, "box", -shift) for shift in range(-reach, reach + 1)], axis=2
        )
        pieces = [[window[trial].reshape(-1, cells_z)] for trial in range(trials_here)]
        planes = 2 * reach + 1
        slot = place * lax.axis_size("trial") + lax.axis_index("trial")
        rows = lax.psum(jnp.where((owners == slot)[:, None, None], store, 0.0), ("box", "trial"))
        rows = rows.reshape(STEPS * 3, all_planes, per).transpose(1, 0, 2)
        rows = jnp.pad(rows, ((reach, reach), (0, LINES - STEPS * 3), (0, 0)))
        rows = lax.dynamic_slice_in_dim(rows, place, planes, 0)
        given = jnp.tile(rows, (1, 1, cells_z // per))
        offsets = jnp.pad(offsets, ((reach, reach), (0, 0)), constant_values=-1)
        offsets = lax.dynamic_slice_in_dim(offsets, place, planes, 0)
        scalars = (place[None], brick_map, owners)
    hots = hot_planes(jnp.tile(offsets, (1, cells_z // per)), cells_y, cells_z)
    shape = (planes, cells_y, cells_z, per)
    before = None
    for trial in range(trials_here):
        found = run_trial(trial, trials_here, shape, scalars, pieces[trial], hots, given, before)
        before = found[:2]
        if trial == 0:
            given = found[2]
    return tuple(before)


def solution(mesh):
    return jax.shard_map(
        per_device,
        mesh=mesh,
        in_specs=(
            P("trial", None, None, "box", None),
            P(("groups", "box", "trial"), None, None),
            P(),
            P(),
            P(),
        ),
        out_specs=(
            P(("groups", "trial"), None, "box", None, None),
            P(("groups", "trial"), None, "box", None, None),
        ),
        check_vma=False,
    )
```

```python
import functools

import jax
import jax.numpy as jnp
from jax import lax
from jax.experimental import pallas as pl
from jax.experimental.pallas import tpu as pltpu
from jax.sharding import PartitionSpec as P

STEPS = 6
TIME_STEP = 0.25
VX, VY, VZ, XX, YY, ZZ, XY, XZ, YZ = range(9)
ROWS = 8
LINES = 24


def ring_place(box, count):
    return jnp.where(box % 2 == 0, box // 2, count - 1 - box // 2)


def ring_box(place, count):
    return jnp.where(place < count // 2, 2 * place, 2 * (count - 1 - place) + 1)


def ring_offsets(count):
    steps = [0]
    for distance in range(1, count // 2):
        steps += [-distance, distance]
    return steps + [count // 2]


def split_values(value, per):
    group = lax.broadcasted_iota(jnp.int32, value.shape, 1) // per
    high = value.astype(jnp.bfloat16).astype(jnp.float32)
    rest = value - high
    middle = rest.astype(jnp.bfloat16).astype(jnp.float32)
    low = rest - middle
    return jnp.where(
        group == 0, high, jnp.where(group == 1, middle, jnp.where(group == 2, low, 0.0))
    )


class Plane:
    def __init__(self, fields, index, cells_y, cells_z):
        self.fields, self.index, self.chunks = fields, index, cells_y // ROWS
        row = lax.broadcasted_iota(jnp.int32, (ROWS, cells_z), 0)
        lane = lax.broadcasted_iota(jnp.int32, (ROWS, cells_z), 1)
        self.first_row, self.last_row = row == 0, row == ROWS - 1
        self.first_lane, self.last_lane = lane == 0, lane == cells_z - 1
        self.cells_z = cells_z
        self.loaded, self.rolled = {}, {}

    def at(self, field, chunk, beside=0):
        if (field, chunk, beside) not in self.loaded:
            self.loaded[field, chunk, beside] = self.fields[field][
                self.index + beside, chunk * ROWS : chunk * ROWS + ROWS, :
            ]
        return self.loaded[field, chunk, beside]

    def put(self, field, chunk, value):
        self.fields[field][self.index, chunk * ROWS : chunk * ROWS + ROWS, :] = value

    def roll_rows(self, field, chunk, by):
        if not 0 <= chunk < self.chunks:
            return 0.0
        if (field, chunk) not in self.rolled:
            self.rolled[field, chunk] = pltpu.roll(self.at(field, chunk), by, 0)
        return self.rolled[field, chunk]

    def back_y(self, field, chunk):
        here = self.roll_rows(field, chunk, 1)
        before = self.roll_rows(field, chunk - 1, 1)
        return self.at(field, chunk) - jnp.where(self.first_row, before, here)

    def fore_y(self, field, chunk):
        here = self.roll_rows(field, chunk, ROWS - 1)
        after = self.roll_rows(field, chunk + 1, ROWS - 1)
        return jnp.where(self.last_row, after, here) - self.at(field, chunk)

    def back_x(self, field, chunk):
        return self.at(field, chunk) - self.at(field, chunk, -1)

    def fore_x(self, field, chunk):
        return self.at(field, chunk, 1) - self.at(field, chunk)

    def back_z(self, field, chunk):
        value = self.at(field, chunk)
        return value - jnp.where(self.first_lane, 0.0, pltpu.roll(value, 1, 1))

    def fore_z(self, field, chunk):
        value = self.at(field, chunk)
        return jnp.where(self.last_lane, 0.0, pltpu.roll(value, self.cells_z - 1, 1)) - value


def propagate(plan, *refs):
    parts, row_parts, ring, planes, cells_y, cells_z, per, first = plan
    refs = list(refs)
    place_ref, map_ref, owners_ref = refs[:3]
    operands = 1 + max(part[0] for part in parts)
    piece_refs = refs[3 : 3 + operands]
    rest = refs[3 + operands :]
    hot_y, hot_z = rest[:2]
    rest = rest[2:]
    if ring == 1 or not first:
        given_ref = rest[0]
        rest = rest[1:]
    if not first:
        rest = rest[2:]
    vel_ref, str_ref = rest[:2]
    rest = rest[2:]
    if first:
        values = rest[0]
        rest = rest[1:]
    else:
        values = given_ref
    fields, (medium, added, stored, lines, sems) = rest[:9], rest[9:]
    block_y = cells_y // ring
    chunks = cells_y // ROWS

    if ring > 1:
        centre = place_ref[0]
        start = ring_place(centre, ring)
        boxes = {
            step: ring_box(lax.rem(start + step + ring, ring), ring) for step in ring_offsets(ring)
        }
        blocks = {step: map_ref[box] for step, box in boxes.items()}
    else:
        centre = planes // 2
        blocks = {0: 0}
    for operand, row, first_unit, units, offset in parts:
        top = pl.multiple_of(blocks[offset] * block_y, 8)
        for unit in range(units):
            component, plane = divmod(first_unit + unit, planes)
            source = row + unit * block_y
            medium[component, plane, pl.ds(top, block_y), :] = (
                TIME_STEP * piece_refs[operand][source : source + block_y, :]
            )

    outside = jnp.zeros((cells_y, cells_z), jnp.float32)
    for field in (XY, XZ, VX):
        fields[field][0] = outside
    for field in (XX, VY, VZ):
        fields[field][planes + 1] = outside

    if first and ring > 1:
        halves = planes * per // cells_z
        for operand, row, offset in row_parts:
            stored[boxes[offset]] = piece_refs[operand][row : row + 2 * ROWS, :]
        for step in range(STEPS):
            owner = owners_ref[step]
            for comp in range(3):
                for half in range(halves):
                    source = (owner % 2) * 3 * halves + comp * halves + half
                    lines[half, pl.ds(step * 3 + comp, 1), :] = stored[owner // 2, pl.ds(source, 1), :]
        for plane in range(planes):
            half, begin = divmod(plane * per, cells_z)
            line = lines[half]
            group = lax.broadcasted_iota(jnp.int32, line.shape, 1) // per
            spread = pltpu.roll(line, cells_z - begin, 1) if begin else line
            spread = jnp.where(
                group == 0,
                spread,
                jnp.where(group == 1, pltpu.roll(spread, per, 1), pltpu.roll(spread, 2 * per, 1)),
            )
            values[plane] = split_values(spread, per)
    elif first:
        for plane in range(planes):
            values[plane] = split_values(given_ref[plane], per)

    def inject(step, plane):
        spots = hot_y[plane]
        rows = [values[plane, pl.ds(step * 3 + comp, 1), :] for comp in range(3)]
        weighted = jnp.concatenate([(spots * row).astype(jnp.bfloat16) for row in rows], axis=0)
        found = jnp.dot(weighted, hot_z[plane], preferred_element_type=jnp.float32)
        return [found[comp * cells_y : comp * cells_y + cells_y] for comp in range(3)]

    def limits(step):
        reach = STEPS - 1 - step
        return jnp.maximum(centre - reach, 0), jnp.minimum(centre + reach, planes - 1)

    def medium_at(component, plane, chunk):
        return medium[component, plane, chunk * ROWS : chunk * ROWS + ROWS, :]

    def added_at(comp, plane, chunk):
        return added[comp, plane, chunk * ROWS : chunk * ROWS + ROWS, :]

    def start_velocity(plane, carry):
        for comp, value in enumerate(inject(0, plane)):
            fields[comp][plane + 1] = value
        return carry

    def velocity(components, plane, carry):
        here = Plane(fields, plane + 1, cells_y, cells_z)
        for chunk in range(chunks):
            gain = medium_at(2, plane, chunk)
            pulls = []
            if VX in components:
                pull = here.fore_x(XX, chunk) + here.back_y(XY, chunk) + here.back_z(XZ, chunk)
                pulls.append((VX, pull))
            if VY in components:
                pull = here.back_x(XY, chunk) + here.fore_y(YY, chunk) + here.back_z(YZ, chunk)
                pulls.append((VY, pull))
            if VZ in components:
                pull = here.back_x(XZ, chunk) + here.back_y(YZ, chunk) + here.fore_z(ZZ, chunk)
                pulls.append((VZ, pull))
            for comp, pull in pulls:
                new = here.at(comp, chunk) + gain * pull
                here.put(comp, chunk, new + added_at(comp, plane, chunk))
        return carry

    def stress(step, fresh, final, plane, carry):
        here = Plane(fields, plane + 1, cells_y, cells_z)
        if not final:
            for comp, value in enumerate(inject(step + 1, plane)):
                added[comp, plane] = value
        for chunk in range(chunks):
            lam, mu = medium_at(0, plane, chunk), medium_at(1, plane, chunk)
            twice = mu + mu
            grad_x, grad_y, grad_z = here.back_x(VX, chunk), here.back_y(VY, chunk), here.back_z(VZ, chunk)
            spread = lam * (grad_x + grad_y + grad_z)
            changes = (
                (XX, spread + twice * grad_x),
                (YY, spread + twice * grad_y),
                (ZZ, spread + twice * grad_z),
                (XY, mu * (here.fore_y(VX, chunk) + here.fore_x(VY, chunk))),
                (XZ, mu * (here.fore_z(VX, chunk) + here.fore_x(VZ, chunk))),
                (YZ, mu * (here.fore_z(VY, chunk) + here.fore_y(VZ, chunk))),
            )
            for field, change in changes:
                here.put(field, chunk, change if fresh else here.at(field, chunk) + change)
        return carry

    def velocities(step):
        low, high = limits(step)
        lax.fori_loop(jnp.maximum(low - 1, 0), low, functools.partial(velocity, (VX,)), 0)
        lax.fori_loop(low, high + 1, functools.partial(velocity, (VX, VY, VZ)), 0)
        lax.fori_loop(high + 1, jnp.minimum(high + 2, planes), functools.partial(velocity, (VY, VZ)), 0)

    low, high = limits(0)
    lax.fori_loop(jnp.maximum(low - 1, 0), jnp.minimum(high + 2, planes), start_velocity, 0)
    lax.fori_loop(low, high + 1, functools.partial(stress, 0, True, False), 0)

    def one_step(step, carry):
        velocities(step)
        low, high = limits(step)
        lax.fori_loop(low, high + 1, functools.partial(stress, step, False, False), 0)
        return carry

    lax.fori_loop(1, STEPS - 1, one_step, 0)
    velocities(STEPS - 1)
    stress(STEPS - 1, False, True, centre, 0)

    trial = place_ref[1]
    copies = []
    for field in range(9):
        target = vel_ref.at[trial, field, 0] if field < 3 else str_ref.at[trial, field - 3, 0]
        copies.append(pltpu.make_async_copy(fields[field].at[centre + 1], target, sems.at[field]))
    for copy in copies:
        copy.start()
    for copy in copies:
        copy.wait()


def run_trial(trials, shape, ring, scalars, found, hots, given, before):
    planes, cells_y, cells_z, per = shape
    pieces, parts, row_parts = found
    first = before is None
    smem, vmem, anywhere = (
        pl.BlockSpec(memory_space=space) for space in (pltpu.SMEM, pltpu.VMEM, pl.ANY)
    )
    operands = list(scalars) + list(pieces) + list(hots)
    specs = [smem] * 3 + [vmem] * (len(operands) - 3)
    if given is not None:
        operands.append(given)
        specs.append(vmem)
    out_shape = [
        jax.ShapeDtypeStruct((trials, 3, 1, cells_y, cells_z), jnp.float32),
        jax.ShapeDtypeStruct((trials, 6, 1, cells_y, cells_z), jnp.float32),
    ]
    out_specs = [anywhere, anywhere]
    aliases = {}
    if first:
        out_shape.append(jax.ShapeDtypeStruct((planes, LINES, cells_z), jnp.float32))
        out_specs.append(vmem)
    else:
        aliases = {len(operands): 0, len(operands) + 1: 1}
        operands += list(before)
        specs += [anywhere, anywhere]
    field = pltpu.VMEM((planes + 2, cells_y, cells_z), jnp.float32)
    return pl.pallas_call(
        functools.partial(propagate, (parts, row_parts, ring, planes, cells_y, cells_z, per, first)),
        out_shape=out_shape,
        in_specs=specs,
        out_specs=out_specs,
        input_output_aliases=aliases,
        scratch_shapes=[field] * 9
        + [
            pltpu.VMEM((3, planes, cells_y, cells_z), jnp.float32),
            pltpu.VMEM((3, planes, cells_y, cells_z), jnp.float32),
            pltpu.VMEM((ring, 2 * ROWS, cells_z), jnp.float32),
            pltpu.VMEM((2, LINES, cells_z), jnp.float32),
            pltpu.SemaphoreType.DMA((9,)),
        ],
        compiler_params=pltpu.CompilerParams(vmem_limit_bytes=40 * 1024 * 1024),
        cost_estimate=pl.CostEstimate(flops=30_000_000, bytes_accessed=5_000_000, transcendentals=0),
    )(*operands)


def from_behind(value, axis, steps):
    count = lax.axis_size(axis)
    leading, last = (max(0, -steps), min(count, count - steps))
    return lax.ppermute(value, axis, [(source, source + steps) for source in range(leading, last)])


def around(medium, store, count):
    lanes = medium.shape[-1]
    group = lax.axis_index("groups")
    order = [2 * place for place in range((count + 1) // 2)]
    order += [box for box in range(count - 1, 0, -1) if box % 2 == 1]
    up = [(order[place], order[(place + 1) % count]) for place in range(count)]
    down = [(target, source) for source, target in up]

    def across(value):
        return lax.ppermute(value, "groups", [(0, 1), (1, 0)])

    mine = store[0].reshape(-1, lanes)
    other = lax.ppermute(mine, "trial", [(0, 1), (1, 0)])
    lower = lax.axis_index("trial") == 0
    rows = [jnp.where(lower, mine, other), jnp.where(lower, other, mine)]
    filler = jnp.zeros(((-2 * mine.shape[0]) % ROWS, lanes), jnp.float32)
    bricks = [lax.dynamic_index_in_dim(medium, which, 0, False).reshape(-1, lanes) for which in (group, 1 - group)]
    size = bricks[0].shape[0]
    third, half = size // 3, size // 2
    units = size // medium.shape[3]
    first = jnp.concatenate([bricks[0]] + rows + [filler])
    later = bricks[1][:third]
    pieces, parts, row_parts = [[first], [bricks[1]]], [[(0, 0, 0, units, 0)], [(0, 0, 0, units, 0)]], [(0, size, 0)]

    def keep(which, piece, entries):
        parts[which] += [(len(pieces[which]),) + entry for entry in entries]
        pieces[which].append(piece)

    forth, back, forth_later, back_later, rests = first, first, later, later, []
    for distance in range(1, count // 2):
        forth, back = lax.ppermute(forth, "box", up), lax.ppermute(back, "box", down)
        forth_later = lax.ppermute(forth_later, "box", up)
        back_later = lax.ppermute(back_later, "box", down)
        rest = across(jnp.concatenate([forth[third:size], back[third:size]]))
        rests.append(rest)
        for piece, offset in ((forth, -distance), (back, distance)):
            row_parts.append((len(pieces[0]), size, offset))
            keep(0, piece, [(0, 0, units, offset)])
        for piece, offset in ((forth_later, -distance), (back_later, distance)):
            keep(1, piece, [(0, 0, units // 3, offset)])
        keep(1, rest, [(0, units // 3, units - units // 3, -distance),
                       (size - third, units // 3, units - units // 3, distance)])
    far = count // 2
    forth, back, _ = lax.optimization_barrier((forth, back, rests[0]))
    forth, back = lax.ppermute(forth[:half], "box", up), lax.ppermute(back[half:], "box", down)
    row_parts.append((len(pieces[0]) + 1, size - half, far))
    keep(0, forth, [(0, 0, units // 2, far)])
    keep(0, back, [(0, units // 2, units - units // 2, far)])
    keep(1, lax.ppermute(forth_later, "box", up), [(0, 0, units // 3, far)])
    rest = across(jnp.concatenate([forth[third:], back[: size - half]]))
    pieces[0][-1], _ = lax.optimization_barrier((pieces[0][-1], rests[1]))
    keep(1, rest, [(0, units // 3, units - units // 3, far)])
    return (pieces[0], parts[0], row_parts), (pieces[1], parts[1], [])


def hot_planes(offsets, cells_y, cells_z):
    rows = jnp.arange(cells_y, dtype=jnp.int32)[None, :, None]
    columns = jnp.arange(cells_z, dtype=jnp.int32)[None, None, :]
    hot_y = (offsets[:, None, :] // cells_z == rows).astype(jnp.float32)
    hot_z = (offsets[:, :, None] % cells_z == columns).astype(jnp.bfloat16)
    return hot_y, hot_z


def per_device(medium, store, surf_off, owners, brick_map):
    boxes = lax.axis_size("box")
    place = lax.axis_index("box")
    trials_here, _, all_planes, brick_y, cells_z = medium.shape
    cells_y = boxes * brick_y
    per = surf_off.shape[0] // all_planes
    offsets = surf_off.reshape(all_planes, per)
    reach = STEPS
    pairs = lax.axis_size("trial") == 2 and lax.axis_size("groups") == 2 and trials_here == 2
    if pairs and boxes == 8 and all_planes == 8:
        ring, planes, given = boxes, all_planes, None
        found = around(medium, store, boxes)
        slots = [lax.axis_index("groups"), 1 - lax.axis_index("groups")]
    else:
        inverse = jnp.zeros((boxes,), jnp.int32).at[brick_map].set(jnp.arange(boxes, dtype=jnp.int32))
        moved = lax.all_to_all(medium, "box", split_axis=2, concat_axis=3, tiled=True)
        blocks = moved.reshape(trials_here, 3, 1, boxes, brick_y, cells_z)
        mine = jnp.take(blocks, inverse, axis=3).reshape(trials_here, 3, 1, cells_y, cells_z)
        window = jnp.concatenate(
            [from_behind(mine, "box", -shift) for shift in range(-reach, reach + 1)], axis=2
        )
        ring, planes = 1, 2 * reach + 1
        found = [
            ([window[trial].reshape(-1, cells_z)], [(0, 0, 0, 3 * planes, 0)], []) for trial in range(trials_here)
        ]
        slot = place * lax.axis_size("trial") + lax.axis_index("trial")
        rows = lax.psum(jnp.where((owners == slot)[:, None, None], store, 0.0), ("box", "trial"))
        rows = rows.reshape(STEPS * 3, all_planes, per).transpose(1, 0, 2)
        rows = jnp.pad(rows, ((reach, reach), (0, LINES - STEPS * 3), (0, 0)))
        rows = lax.dynamic_slice_in_dim(rows, place, planes, 0)
        given = jnp.tile(rows, (1, 1, cells_z // per))
        offsets = jnp.pad(offsets, ((reach, reach), (0, 0)), constant_values=-1)
        offsets = lax.dynamic_slice_in_dim(offsets, place, planes, 0)
        slots = list(range(trials_here))
    hots = hot_planes(jnp.tile(offsets, (1, cells_z // per)), cells_y, cells_z)
    shape = (planes, cells_y, cells_z, per)
    before = None
    for trial in range(trials_here):
        geometry = jnp.stack([place, jnp.int32(slots[trial])])
        scalars = (geometry, brick_map, owners)
        results = run_trial(trials_here, shape, ring, scalars, found[trial], hots, given, before)
        before = results[:2]
        if trial == 0:
            given = results[2]
    return tuple(before)


def solution(mesh):
    return jax.shard_map(
        per_device,
        mesh=mesh,
        in_specs=(
            P("trial", None, None, "box", None),
            P(("groups", "box", "trial"), None, None),
            P(),
            P(),
            P(),
        ),
        out_specs=(
            P(("groups", "trial"), None, "box", None, None),
            P(("groups", "trial"), None, "box", None, None),
        ),
        check_vma=False,
    )
```

```python
import functools

import jax
import jax.numpy as jnp
from jax import lax
from jax.experimental import pallas as pl
from jax.experimental.pallas import tpu as pltpu
from jax.sharding import PartitionSpec as P

STEPS = 6
TIME_STEP = 0.25
VX, VY, VZ, XX, YY, ZZ, XY, XZ, YZ = range(9)
ROWS = 8
LINES = 24
GROUP = 4


def ring_place(box, count):
    return jnp.where(box % 2 == 0, box // 2, count - 1 - box // 2)


def ring_box(place, count):
    return jnp.where(place < count // 2, 2 * place, 2 * (count - 1 - place) + 1)


def ring_offsets(count):
    steps = [0]
    for distance in range(1, count // 2):
        steps += [-distance, distance]
    return steps + [count // 2]


def split_values(value, per):
    group = lax.broadcasted_iota(jnp.int32, value.shape, 1) // per
    high = value.astype(jnp.bfloat16).astype(jnp.float32)
    rest = value - high
    middle = rest.astype(jnp.bfloat16).astype(jnp.float32)
    low = rest - middle
    return jnp.where(
        group == 0, high, jnp.where(group == 1, middle, jnp.where(group == 2, low, 0.0))
    )


class Plane:
    def __init__(self, sources, cells_y, cells_z):
        self.sources, self.chunks = sources, cells_y // ROWS
        row = lax.broadcasted_iota(jnp.int32, (ROWS, cells_z), 0)
        lane = lax.broadcasted_iota(jnp.int32, (ROWS, cells_z), 1)
        self.first_row, self.last_row = row == 0, row == ROWS - 1
        self.first_lane, self.last_lane = lane == 0, lane == cells_z - 1
        self.cells_z = cells_z
        self.loaded, self.rolled = {}, {}

    def fetch(self, chunk):
        if chunk < self.chunks:
            for name, (array, lead) in self.sources.items():
                self.loaded[name, chunk] = array[lead + (slice(chunk * ROWS, chunk * ROWS + ROWS),)]

    def at(self, name, chunk, beside=0):
        return self.loaded[(name, beside) if beside else name, chunk]

    def put(self, name, chunk, value):
        array, lead = self.sources[name]
        array[lead + (slice(chunk * ROWS, chunk * ROWS + ROWS),)] = value

    def roll_rows(self, field, chunk, by):
        if not 0 <= chunk < self.chunks:
            return 0.0
        if (field, chunk) not in self.rolled:
            self.rolled[field, chunk] = pltpu.roll(self.at(field, chunk), by, 0)
        return self.rolled[field, chunk]

    def back_y(self, field, chunk):
        here = self.roll_rows(field, chunk, 1)
        before = self.roll_rows(field, chunk - 1, 1)
        return self.at(field, chunk) - jnp.where(self.first_row, before, here)

    def fore_y(self, field, chunk):
        here = self.roll_rows(field, chunk, ROWS - 1)
        after = self.roll_rows(field, chunk + 1, ROWS - 1)
        return jnp.where(self.last_row, after, here) - self.at(field, chunk)

    def back_x(self, field, chunk):
        return self.at(field, chunk) - self.at(field, chunk, -1)

    def fore_x(self, field, chunk):
        return self.at(field, chunk, 1) - self.at(field, chunk)

    def back_z(self, field, chunk):
        value = self.at(field, chunk)
        return value - jnp.where(self.first_lane, 0.0, pltpu.roll(value, 1, 1))

    def fore_z(self, field, chunk):
        value = self.at(field, chunk)
        return jnp.where(self.last_lane, 0.0, pltpu.roll(value, self.cells_z - 1, 1)) - value


def propagate(plan, *refs):
    parts, row_parts, ring, planes, cells_y, cells_z, per, first = plan
    refs = list(refs)
    scalars = refs[0]
    operands = 1 + max(part[0] for part in parts)
    piece_refs = refs[1 : 1 + operands]
    rest = refs[1 + operands :]
    hot_y, hot_z = rest[:2]
    rest = rest[2:]
    if ring == 1 or not first:
        given_ref = rest[0]
        rest = rest[1:]
    if not first:
        rest = rest[2:]
    vel_ref, str_ref = rest[:2]
    rest = rest[2:]
    if first:
        values = rest[0]
        rest = rest[1:]
    else:
        values = given_ref
    fields, (medium, added, stored, lines, sems) = rest[:9], rest[9:]
    block_y = cells_y // ring
    chunks = cells_y // ROWS

    if ring > 1:
        centre = scalars[0]
        start = ring_place(centre, ring)
        boxes = {
            step: ring_box(lax.rem(start + step + ring, ring), ring) for step in ring_offsets(ring)
        }
        blocks = {step: scalars[2 + box] for step, box in boxes.items()}
    else:
        centre = planes // 2
        blocks = {0: 0}
    for operand, row, first_unit, units, offset in parts:
        top = pl.multiple_of(blocks[offset] * block_y, 8)
        for unit in range(units):
            component, plane = divmod(first_unit + unit, planes)
            source = row + unit * block_y
            medium[component, plane, pl.ds(top, block_y), :] = (
                TIME_STEP * piece_refs[operand][source : source + block_y, :]
            )

    outside = jnp.zeros((cells_y, cells_z), jnp.float32)
    for field in (XY, XZ, VX):
        fields[field][0] = outside
    for field in (XX, VY, VZ):
        fields[field][planes + 1] = outside

    if first and ring > 1:
        halves = planes * per // cells_z
        for operand, row, offset in row_parts:
            stored[boxes[offset]] = piece_refs[operand][row : row + 2 * ROWS, :]
        for step in range(STEPS):
            owner = scalars[2 + ring + step]
            for comp in range(3):
                for half in range(halves):
                    source = (owner % 2) * 3 * halves + comp * halves + half
                    lines[half, pl.ds(step * 3 + comp, 1), :] = stored[owner // 2, pl.ds(source, 1), :]
        for plane in range(planes):
            half, begin = divmod(plane * per, cells_z)
            line = lines[half]
            group = lax.broadcasted_iota(jnp.int32, line.shape, 1) // per
            spread = pltpu.roll(line, cells_z - begin, 1) if begin else line
            spread = jnp.where(
                group == 0,
                spread,
                jnp.where(group == 1, pltpu.roll(spread, per, 1), pltpu.roll(spread, 2 * per, 1)),
            )
            values[plane] = split_values(spread, per)
    elif first:
        for plane in range(planes):
            values[plane] = split_values(given_ref[plane], per)

    def inject(step, plane, begin, size):
        spots = hot_y[plane, begin : begin + size]
        rows = [values[plane, pl.ds(step * 3 + comp, 1), :] for comp in range(3)]
        weighted = jnp.concatenate([(spots * row).astype(jnp.bfloat16) for row in rows], axis=0)
        found = jnp.dot(weighted, hot_z[plane], preferred_element_type=jnp.float32)
        return [found[comp * size : comp * size + size] for comp in range(3)]

    def limits(step):
        reach = STEPS - 1 - step
        return jnp.maximum(centre - reach, 0), jnp.minimum(centre + reach, planes - 1)

    def beside(field, index, step=0):
        return fields[field], (index + step,)

    def velocity(components, plane, carry):
        index = plane + 1
        sources = {"gain": (medium, (2, plane))}
        for field in components:
            sources[field] = beside(field, index)
            sources["added", field] = (added, (field, plane))
        if VX in components:
            sources.update({XX: beside(XX, index), (XX, 1): beside(XX, index, 1)})
        if VY in components:
            sources.update({(XY, -1): beside(XY, index, -1), YY: beside(YY, index)})
        if VZ in components:
            sources.update({(XZ, -1): beside(XZ, index, -1), ZZ: beside(ZZ, index)})
        if VY in components or VZ in components:
            sources[YZ] = beside(YZ, index)
        sources.update({XY: beside(XY, index), XZ: beside(XZ, index)})
        here = Plane(sources, cells_y, cells_z)
        here.fetch(0)
        for chunk in range(chunks):
            here.fetch(chunk + 1)
            gain = here.at("gain", chunk)
            pulls = []
            if VX in components:
                pull = here.fore_x(XX, chunk) + here.back_y(XY, chunk) + here.back_z(XZ, chunk)
                pulls.append((VX, pull))
            if VY in components:
                pull = here.back_x(XY, chunk) + here.fore_y(YY, chunk) + here.back_z(YZ, chunk)
                pulls.append((VY, pull))
            if VZ in components:
                pull = here.back_x(XZ, chunk) + here.back_y(YZ, chunk) + here.fore_z(ZZ, chunk)
                pulls.append((VZ, pull))
            news = [
                (comp, here.at(comp, chunk) + gain * pull + here.at(("added", comp), chunk))
                for comp, pull in pulls
            ]
            for comp, new in news:
                here.put(comp, chunk, new)
        return carry

    def stress(step, fresh, final, plane, carry):
        index = plane + 1
        sources = {"lam": (medium, (0, plane)), "mu": (medium, (1, plane))}
        sources.update({field: beside(field, index) for field in range(3 if fresh else 9)})
        sources.update({(field, by): beside(field, index, by) for field, by in ((VX, -1), (VY, 1), (VZ, 1))})
        if fresh:
            targets = Plane({field: beside(field, index) for field in range(3, 9)}, cells_y, cells_z)
        here = Plane(sources, cells_y, cells_z)
        here.fetch(0)
        for chunk in range(chunks):
            if not final and chunk % GROUP == 0:
                begin = chunk * ROWS
                found = inject(step + 1, plane, begin, GROUP * ROWS)
            here.fetch(chunk + 1)
            lam, mu = here.at("lam", chunk), here.at("mu", chunk)
            twice = mu + mu
            grad_x, grad_y, grad_z = here.back_x(VX, chunk), here.back_y(VY, chunk), here.back_z(VZ, chunk)
            spread = lam * (grad_x + grad_y + grad_z)
            changes = (
                (XX, spread + twice * grad_x),
                (YY, spread + twice * grad_y),
                (ZZ, spread + twice * grad_z),
                (XY, mu * (here.fore_y(VX, chunk) + here.fore_x(VY, chunk))),
                (XZ, mu * (here.fore_z(VX, chunk) + here.fore_x(VZ, chunk))),
                (YZ, mu * (here.fore_z(VY, chunk) + here.fore_y(VZ, chunk))),
            )
            if fresh:
                for field, change in changes:
                    targets.put(field, chunk, change)
            else:
                news = [(field, here.at(field, chunk) + change) for field, change in changes]
                for field, new in news:
                    here.put(field, chunk, new)
            if not final and chunk % GROUP == GROUP - 1:
                for comp, value in enumerate(found):
                    added[comp, plane, begin : begin + GROUP * ROWS] = value
        return carry

    def velocities(step):
        low, high = limits(step)
        lax.fori_loop(jnp.maximum(low - 1, 0), low, functools.partial(velocity, (VX,)), 0)
        lax.fori_loop(low, high + 1, functools.partial(velocity, (VX, VY, VZ)), 0)
        lax.fori_loop(high + 1, jnp.minimum(high + 2, planes), functools.partial(velocity, (VY, VZ)), 0)

    for plane in range(planes):
        for comp, value in enumerate(inject(0, plane, 0, cells_y)):
            fields[comp][plane + 1] = value
    low, high = limits(0)
    lax.fori_loop(low, high + 1, functools.partial(stress, 0, True, False), 0)

    def one_step(step, carry):
        velocities(step)
        low, high = limits(step)
        lax.fori_loop(low, high + 1, functools.partial(stress, step, False, False), 0)
        return carry

    lax.fori_loop(1, STEPS - 1, one_step, 0)
    trial = scalars[1]
    copies = []
    for field in range(9):
        target = vel_ref.at[trial, field, 0] if field < 3 else str_ref.at[trial, field - 3, 0]
        copies.append(pltpu.make_async_copy(fields[field].at[centre + 1], target, sems.at[field]))
    velocities(STEPS - 1)
    for copy in copies[:3]:
        copy.start()
    stress(STEPS - 1, False, True, centre, 0)
    for copy in copies[3:]:
        copy.start()
    for copy in copies:
        copy.wait()


def run_trial(trials, shape, ring, scalars, found, hots, given, before):
    planes, cells_y, cells_z, per = shape
    pieces, parts, row_parts = found
    first = before is None
    smem, vmem, anywhere = (
        pl.BlockSpec(memory_space=space) for space in (pltpu.SMEM, pltpu.VMEM, pl.ANY)
    )
    operands = [scalars] + list(pieces) + list(hots)
    specs = [smem] + [vmem] * (len(operands) - 1)
    if given is not None:
        operands.append(given)
        specs.append(vmem)
    out_shape = [
        jax.ShapeDtypeStruct((trials, 3, 1, cells_y, cells_z), jnp.float32),
        jax.ShapeDtypeStruct((trials, 6, 1, cells_y, cells_z), jnp.float32),
    ]
    out_specs = [anywhere, anywhere]
    aliases = {}
    if first:
        out_shape.append(jax.ShapeDtypeStruct((planes, LINES, cells_z), jnp.float32))
        out_specs.append(vmem)
    else:
        aliases = {len(operands): 0, len(operands) + 1: 1}
        operands += list(before)
        specs += [anywhere, anywhere]
    field = pltpu.VMEM((planes + 2, cells_y, cells_z), jnp.float32)
    return pl.pallas_call(
        functools.partial(propagate, (parts, row_parts, ring, planes, cells_y, cells_z, per, first)),
        out_shape=out_shape,
        in_specs=specs,
        out_specs=out_specs,
        input_output_aliases=aliases,
        scratch_shapes=[field] * 9
        + [
            pltpu.VMEM((3, planes, cells_y, cells_z), jnp.float32),
            pltpu.VMEM((3, planes, cells_y, cells_z), jnp.float32),
            pltpu.VMEM((ring, 2 * ROWS, cells_z), jnp.float32),
            pltpu.VMEM((2, LINES, cells_z), jnp.float32),
            pltpu.SemaphoreType.DMA((9,)),
        ],
        compiler_params=pltpu.CompilerParams(vmem_limit_bytes=24 * 1024 * 1024),
        cost_estimate=pl.CostEstimate(flops=1_000_000, bytes_accessed=100_000, transcendentals=0),
    )(*operands)


def from_behind(value, axis, steps):
    count = lax.axis_size(axis)
    leading, last = (max(0, -steps), min(count, count - steps))
    return lax.ppermute(value, axis, [(source, source + steps) for source in range(leading, last)])


def around(medium, store, early, count):
    lanes = medium.shape[-1]
    group = lax.axis_index("groups")
    order = [2 * place for place in range((count + 1) // 2)]
    order += [box for box in range(count - 1, 0, -1) if box % 2 == 1]
    up = [(order[place], order[(place + 1) % count]) for place in range(count)]
    down = [(target, source) for source, target in up]

    def across(value):
        return lax.ppermute(value, "groups", [(0, 1), (1, 0)])

    mine = store[0].reshape(-1, lanes)
    other = lax.ppermute(mine, "trial", [(0, 1), (1, 0)])
    lower = lax.axis_index("trial") == 0
    rows = [jnp.where(lower, mine, other), jnp.where(lower, other, mine)]
    filler = jnp.zeros(((-2 * mine.shape[0]) % ROWS, lanes), jnp.float32)
    bricks = [lax.dynamic_index_in_dim(medium, which, 0, False).reshape(-1, lanes) for which in (group, 1 - group)]
    size = bricks[0].shape[0]
    third, half = size // 3, size // 2
    units = size // medium.shape[3]
    first = jnp.concatenate([bricks[0]] + rows + [filler])
    later = bricks[1][:third]
    pieces, parts, row_parts = [[first], [bricks[1]]], [[(0, 0, 0, units, 0)], [(0, 0, 0, units, 0)]], [(0, size, 0)]

    def keep(which, piece, entries):
        parts[which] += [(len(pieces[which]),) + entry for entry in entries]
        pieces[which].append(piece)

    forth, back, forth_later, back_later, rests = first, first, later, later, []
    lates = []
    for distance in range(1, count // 2):
        if distance == 3:
            forth, early = lax.optimization_barrier((forth, early))
        forth, back = lax.ppermute(forth, "box", up), lax.ppermute(back, "box", down)
        for piece, offset in ((forth, -distance), (back, distance)):
            row_parts.append((len(pieces[0]), size, offset))
            keep(0, piece, [(0, 0, units, offset)])
        skip = 0
        if distance < 3:
            skip = third
            forth_later = lax.ppermute(forth_later, "box", up)
            back_later = lax.ppermute(back_later, "box", down)
            lates.append((forth_later, back_later))
            for piece, offset in ((forth_later, -distance), (back_later, distance)):
                keep(1, piece, [(0, 0, units // 3, offset)])
        left = units - skip * units // size
        rest = across(jnp.concatenate([forth[skip:size], back[skip:size]]))
        rests.append(rest)
        keep(1, rest, [(0, units - left, left, -distance), (size - skip, units - left, left, distance)])
    far = count // 2
    forth, back, _ = lax.optimization_barrier((forth, back, (rests[:2], lates[0])))
    forth, back = lax.ppermute(forth[:half], "box", up), lax.ppermute(back[half:], "box", down)
    row_parts.append((len(pieces[0]) + 1, size - half, far))
    keep(0, forth, [(0, 0, units // 2, far)])
    keep(0, back, [(0, units // 2, units - units // 2, far)])
    rest = across(jnp.concatenate([forth, back[: size - half]]))
    keep(1, rest, [(0, 0, units, far)])
    return ((pieces[0], parts[0], row_parts), (pieces[1], parts[1], [])), early


def hot_planes(offsets, cells_y, cells_z):
    rows = jnp.arange(cells_y, dtype=jnp.int32)[None, :, None]
    columns = jnp.arange(cells_z, dtype=jnp.int32)[None, None, :]
    hot_y = (offsets[:, None, :] // cells_z == rows).astype(jnp.float32)
    hot_z = (offsets[:, :, None] % cells_z == columns).astype(jnp.bfloat16)
    return hot_y, hot_z


def per_device(medium, store, surf_off, owners, brick_map):
    boxes = lax.axis_size("box")
    place = lax.axis_index("box")
    trials_here, _, all_planes, brick_y, cells_z = medium.shape
    cells_y = boxes * brick_y
    per = surf_off.shape[0] // all_planes
    offsets = surf_off.reshape(all_planes, per)
    reach = STEPS
    pairs = lax.axis_size("trial") == 2 and lax.axis_size("groups") == 2 and trials_here == 2
    if pairs and boxes == 8 and all_planes == 8:
        ring, planes, given = boxes, all_planes, None
        group = lax.axis_index("groups")
        hots = hot_planes(jnp.tile(offsets, (1, cells_z // per)), cells_y, cells_z)
        scalars = [
            jnp.concatenate([jnp.stack([place, slot]), brick_map, owners]) for slot in (group, 1 - group)
        ]
        found, (hots, scalars) = around(medium, store, (hots, scalars), boxes)
    else:
        inverse = jnp.zeros((boxes,), jnp.int32).at[brick_map].set(jnp.arange(boxes, dtype=jnp.int32))
        moved = lax.all_to_all(medium, "box", split_axis=2, concat_axis=3, tiled=True)
        blocks = moved.reshape(trials_here, 3, 1, boxes, brick_y, cells_z)
        mine = jnp.take(blocks, inverse, axis=3).reshape(trials_here, 3, 1, cells_y, cells_z)
        window = jnp.concatenate(
            [from_behind(mine, "box", -shift) for shift in range(-reach, reach + 1)], axis=2
        )
        ring, planes = 1, 2 * reach + 1
        found = [
            ([window[trial].reshape(-1, cells_z)], [(0, 0, 0, 3 * planes, 0)], []) for trial in range(trials_here)
        ]
        slot = place * lax.axis_size("trial") + lax.axis_index("trial")
        rows = lax.psum(jnp.where((owners == slot)[:, None, None], store, 0.0), ("box", "trial"))
        rows = rows.reshape(STEPS * 3, all_planes, per).transpose(1, 0, 2)
        rows = jnp.pad(rows, ((reach, reach), (0, LINES - STEPS * 3), (0, 0)))
        rows = lax.dynamic_slice_in_dim(rows, place, planes, 0)
        given = jnp.tile(rows, (1, 1, cells_z // per))
        offsets = jnp.pad(offsets, ((reach, reach), (0, 0)), constant_values=-1)
        offsets = lax.dynamic_slice_in_dim(offsets, place, planes, 0)
        hots = hot_planes(jnp.tile(offsets, (1, cells_z // per)), cells_y, cells_z)
        scalars = [jnp.stack([place, jnp.int32(trial)]) for trial in range(trials_here)]
    shape = (planes, cells_y, cells_z, per)
    before = None
    for trial in range(trials_here):
        results = run_trial(trials_here, shape, ring, scalars[trial], found[trial], hots, given, before)
        before = results[:2]
        if trial == 0:
            given = results[2]
    return tuple(before)


def solution(mesh):
    return jax.shard_map(
        per_device,
        mesh=mesh,
        in_specs=(
            P("trial", None, None, "box", None),
            P(("groups", "box", "trial"), None, None),
            P(),
            P(),
            P(),
        ),
        out_specs=(
            P(("groups", "trial"), None, "box", None, None),
            P(("groups", "trial"), None, "box", None, None),
        ),
        check_vma=False,
    )
```

```python
import functools

import jax
import jax.numpy as jnp
from jax import lax
from jax.experimental import pallas as pl
from jax.experimental.pallas import tpu as pltpu
from jax.sharding import PartitionSpec as P

STEPS = 6
TIME_STEP = 0.25
VX, VY, VZ, XX, YY, ZZ, XY, XZ, YZ = range(9)
ROWS = 8
LINES = 24
GROUP = 4


def ring_place(box, count):
    return jnp.where(box % 2 == 0, box // 2, count - 1 - box // 2)


def ring_box(place, count):
    return jnp.where(place < count // 2, 2 * place, 2 * (count - 1 - place) + 1)


def ring_offsets(count):
    steps = [0]
    for distance in range(1, count // 2):
        steps += [-distance, distance]
    return steps + [count // 2]


def split_values(value, per):
    group = lax.broadcasted_iota(jnp.int32, value.shape, 1) // per
    high = value.astype(jnp.bfloat16).astype(jnp.float32)
    rest = value - high
    middle = rest.astype(jnp.bfloat16).astype(jnp.float32)
    low = rest - middle
    return jnp.where(
        group == 0, high, jnp.where(group == 1, middle, jnp.where(group == 2, low, 0.0))
    )


class Plane:
    def __init__(self, sources, cells_y, cells_z):
        self.sources, self.chunks = sources, cells_y // ROWS
        row = lax.broadcasted_iota(jnp.int32, (ROWS, cells_z), 0)
        lane = lax.broadcasted_iota(jnp.int32, (ROWS, cells_z), 1)
        self.first_row, self.last_row = row == 0, row == ROWS - 1
        self.first_lane, self.last_lane = lane == 0, lane == cells_z - 1
        self.cells_z = cells_z
        self.loaded = {}

    def fetch(self, chunk):
        if chunk < self.chunks:
            for name, (array, lead) in self.sources.items():
                self.loaded[name, chunk] = array[lead + (slice(chunk * ROWS, chunk * ROWS + ROWS),)]

    def at(self, name, chunk, beside=0):
        return self.loaded[(name, beside) if beside else name, chunk]

    def put(self, name, chunk, value):
        array, lead = self.sources[name]
        array[lead + (slice(chunk * ROWS, chunk * ROWS + ROWS),)] = value

    def edge(self, name, chunk, by):
        array, lead = self.sources[name]
        return pltpu.roll(array[lead + (slice(chunk * ROWS, chunk * ROWS + ROWS),)], by, 0)

    def back_y(self, field, chunk):
        if chunk > 0:
            before = self.at(field, chunk - 1)
        else:
            before = jnp.where(self.first_row, 0.0, self.edge(field, self.chunks - 1, 1))
        return self.at(field, chunk) - before

    def fore_y(self, field, chunk):
        if chunk < self.chunks - 1:
            after = self.at(field, chunk + 1)
        else:
            after = jnp.where(self.last_row, 0.0, self.edge(field, 0, ROWS - 1))
        return after - self.at(field, chunk)

    def back_x(self, field, chunk):
        return self.at(field, chunk) - self.at(field, chunk, -1)

    def fore_x(self, field, chunk):
        return self.at(field, chunk, 1) - self.at(field, chunk)

    def back_z(self, field, chunk):
        value = self.at(field, chunk)
        return value - jnp.where(self.first_lane, 0.0, pltpu.roll(value, 1, 1))

    def fore_z(self, field, chunk):
        value = self.at(field, chunk)
        return jnp.where(self.last_lane, 0.0, pltpu.roll(value, self.cells_z - 1, 1)) - value


def propagate(plan, *refs):
    parts, row_parts, ring, planes, cells_y, cells_z, per, first = plan
    refs = list(refs)
    scalars = refs[0]
    operands = 1 + max(part[0] for part in parts)
    piece_refs = refs[1 : 1 + operands]
    rest = refs[1 + operands :]
    hot_y, hot_z = rest[:2]
    rest = rest[2:]
    if ring == 1 or not first:
        given_ref = rest[0]
        rest = rest[1:]
    if not first:
        rest = rest[2:]
    vel_ref, str_ref = rest[:2]
    rest = rest[2:]
    if first:
        values = rest[0]
        rest = rest[1:]
    else:
        values = given_ref
    fields, (medium, added, stored, lines, results, sems) = rest[:9], rest[9:]
    block_y = cells_y // ring
    chunks = cells_y // ROWS

    if ring > 1:
        centre = scalars[0]
        start = ring_place(centre, ring)
        boxes = {
            step: ring_box(lax.rem(start + step + ring, ring), ring) for step in ring_offsets(ring)
        }
        blocks = {step: scalars[2 + box] for step, box in boxes.items()}
    else:
        centre = planes // 2
        blocks = {0: 0}
    for operand, row, first_unit, units, offset in parts:
        for unit in range(units):
            component, plane = divmod(first_unit + unit, planes)
            for part in range(block_y // chunks):
                source = row + unit * block_y + part * chunks
                line = blocks[offset] * (block_y // chunks) + part
                medium[component, plane, pl.ds(line, chunks, stride=ROWS), :] = (
                    TIME_STEP * piece_refs[operand][source : source + chunks, :]
                )

    outside = jnp.zeros((cells_y, cells_z), jnp.float32)
    for field in (XY, XZ, VX):
        fields[field][0] = outside
    for field in (XX, VY, VZ):
        fields[field][planes + 1] = outside

    if first and ring > 1:
        halves = planes * per // cells_z
        for operand, row, offset in row_parts:
            stored[boxes[offset]] = piece_refs[operand][row : row + 2 * ROWS, :]
        for step in range(STEPS):
            owner = scalars[2 + ring + step]
            for comp in range(3):
                for half in range(halves):
                    source = (owner % 2) * 3 * halves + comp * halves + half
                    lines[half, pl.ds(step * 3 + comp, 1), :] = stored[owner // 2, pl.ds(source, 1), :]
        for plane in range(planes):
            half, begin = divmod(plane * per, cells_z)
            line = lines[half]
            group = lax.broadcasted_iota(jnp.int32, line.shape, 1) // per
            spread = pltpu.roll(line, cells_z - begin, 1) if begin else line
            spread = jnp.where(
                group == 0,
                spread,
                jnp.where(group == 1, pltpu.roll(spread, per, 1), pltpu.roll(spread, 2 * per, 1)),
            )
            values[plane] = split_values(spread, per)
    elif first:
        for plane in range(planes):
            values[plane] = split_values(given_ref[plane], per)

    def inject(step, plane, begin, size):
        spots = hot_y[plane, begin : begin + size]
        rows = [values[plane, pl.ds(step * 3 + comp, 1), :] for comp in range(3)]
        weighted = jnp.concatenate([(spots * row).astype(jnp.bfloat16) for row in rows], axis=0)
        found = jnp.dot(weighted, hot_z[plane], preferred_element_type=jnp.float32)
        return [found[comp * size : comp * size + size] for comp in range(3)]

    def limits(step):
        reach = STEPS - 1 - step
        return jnp.maximum(centre - reach, 0), jnp.minimum(centre + reach, planes - 1)

    def beside(field, index, step=0):
        return fields[field], (index + step,)

    def velocity(components, plane, carry):
        index = plane + 1
        sources = {"gain": (medium, (2, plane))}
        for field in components:
            sources[field] = beside(field, index)
            sources["added", field] = (added, (field, plane))
        if VX in components:
            sources.update({XX: beside(XX, index), (XX, 1): beside(XX, index, 1)})
        if VY in components:
            sources.update({(XY, -1): beside(XY, index, -1), YY: beside(YY, index)})
        if VZ in components:
            sources.update({(XZ, -1): beside(XZ, index, -1), ZZ: beside(ZZ, index)})
        if VY in components or VZ in components:
            sources[YZ] = beside(YZ, index)
        sources.update({XY: beside(XY, index), XZ: beside(XZ, index)})
        here = Plane(sources, cells_y, cells_z)
        here.fetch(0)
        for chunk in range(chunks):
            here.fetch(chunk + 1)
            gain = here.at("gain", chunk)
            pulls = []
            if VX in components:
                pull = here.fore_x(XX, chunk) + here.back_y(XY, chunk) + here.back_z(XZ, chunk)
                pulls.append((VX, pull))
            if VY in components:
                pull = here.back_x(XY, chunk) + here.fore_y(YY, chunk) + here.back_z(YZ, chunk)
                pulls.append((VY, pull))
            if VZ in components:
                pull = here.back_x(XZ, chunk) + here.back_y(YZ, chunk) + here.fore_z(ZZ, chunk)
                pulls.append((VZ, pull))
            news = [
                (comp, here.at(comp, chunk) + gain * pull + here.at(("added", comp), chunk))
                for comp, pull in pulls
            ]
            for comp, new in news:
                here.put(comp, chunk, new)
        return carry

    def stress(step, fresh, final, plane, carry):
        index = plane + 1
        sources = {"lam": (medium, (0, plane)), "mu": (medium, (1, plane))}
        sources.update({field: beside(field, index) for field in range(3 if fresh else 9)})
        sources.update({(field, by): beside(field, index, by) for field, by in ((VX, -1), (VY, 1), (VZ, 1))})
        if fresh:
            targets = Plane({field: beside(field, index) for field in range(3, 9)}, cells_y, cells_z)
        here = Plane(sources, cells_y, cells_z)
        here.fetch(0)
        for chunk in range(chunks):
            if not final and chunk % GROUP == 0:
                begin = chunk * ROWS
                found = inject(step + 1, plane, begin, GROUP * ROWS)
            here.fetch(chunk + 1)
            lam, mu = here.at("lam", chunk), here.at("mu", chunk)
            twice = mu + mu
            grad_x, grad_y, grad_z = here.back_x(VX, chunk), here.back_y(VY, chunk), here.back_z(VZ, chunk)
            spread = lam * (grad_x + grad_y + grad_z)
            changes = (
                (XX, spread + twice * grad_x),
                (YY, spread + twice * grad_y),
                (ZZ, spread + twice * grad_z),
                (XY, mu * (here.fore_y(VX, chunk) + here.fore_x(VY, chunk))),
                (XZ, mu * (here.fore_z(VX, chunk) + here.fore_x(VZ, chunk))),
                (YZ, mu * (here.fore_z(VY, chunk) + here.fore_y(VZ, chunk))),
            )
            if fresh:
                for field, change in changes:
                    targets.put(field, chunk, change)
            else:
                news = [(field, here.at(field, chunk) + change) for field, change in changes]
                for field, new in news:
                    here.put(field, chunk, new)
            if not final and chunk % GROUP == GROUP - 1:
                for comp, value in enumerate(found):
                    added[comp, plane, begin : begin + GROUP * ROWS] = value
        return carry

    def velocities(step):
        low, high = limits(step)
        lax.fori_loop(jnp.maximum(low - 1, 0), low, functools.partial(velocity, (VX,)), 0)
        lax.fori_loop(low, high + 1, functools.partial(velocity, (VX, VY, VZ)), 0)
        lax.fori_loop(high + 1, jnp.minimum(high + 2, planes), functools.partial(velocity, (VY, VZ)), 0)

    for plane in range(planes):
        for comp, value in enumerate(inject(0, plane, 0, cells_y)):
            fields[comp][plane + 1] = value
    low, high = limits(0)
    lax.fori_loop(low, high + 1, functools.partial(stress, 0, True, False), 0)

    def one_step(step, carry):
        velocities(step)
        low, high = limits(step)
        lax.fori_loop(low, high + 1, functools.partial(stress, step, False, False), 0)
        return carry

    lax.fori_loop(1, STEPS - 1, one_step, 0)
    trial = scalars[1]
    copies = []

    def give(field):
        for chunk in range(chunks):
            found = fields[field][centre + 1, chunk * ROWS : chunk * ROWS + ROWS, :]
            results[field, pl.ds(chunk, ROWS, stride=chunks), :] = found
        target = vel_ref.at[trial, field, 0] if field < 3 else str_ref.at[trial, field - 3, 0]
        copies.append(pltpu.make_async_copy(results.at[field], target, sems.at[field]))
        copies[-1].start()

    velocities(STEPS - 1)
    for field in range(3):
        give(field)
    stress(STEPS - 1, False, True, centre, 0)
    for field in range(3, 9):
        give(field)
    for copy in copies:
        copy.wait()


def run_trial(trials, shape, ring, scalars, found, hots, given, before):
    planes, cells_y, cells_z, per = shape
    pieces, parts, row_parts = found
    first = before is None
    smem, vmem, anywhere = (
        pl.BlockSpec(memory_space=space) for space in (pltpu.SMEM, pltpu.VMEM, pl.ANY)
    )
    operands = [scalars] + list(pieces) + list(hots)
    specs = [smem] + [vmem] * (len(operands) - 1)
    if given is not None:
        operands.append(given)
        specs.append(vmem)
    out_shape = [
        jax.ShapeDtypeStruct((trials, 3, 1, cells_y, cells_z), jnp.float32),
        jax.ShapeDtypeStruct((trials, 6, 1, cells_y, cells_z), jnp.float32),
    ]
    out_specs = [anywhere, anywhere]
    aliases = {}
    if first:
        out_shape.append(jax.ShapeDtypeStruct((planes, LINES, cells_z), jnp.float32))
        out_specs.append(vmem)
    else:
        aliases = {len(operands): 0, len(operands) + 1: 1}
        operands += list(before)
        specs += [anywhere, anywhere]
    field = pltpu.VMEM((planes + 2, cells_y, cells_z), jnp.float32)
    return pl.pallas_call(
        functools.partial(propagate, (parts, row_parts, ring, planes, cells_y, cells_z, per, first)),
        out_shape=out_shape,
        in_specs=specs,
        out_specs=out_specs,
        input_output_aliases=aliases,
        scratch_shapes=[field] * 9
        + [
            pltpu.VMEM((3, planes, cells_y, cells_z), jnp.float32),
            pltpu.VMEM((3, planes, cells_y, cells_z), jnp.float32),
            pltpu.VMEM((ring, 2 * ROWS, cells_z), jnp.float32),
            pltpu.VMEM((2, LINES, cells_z), jnp.float32),
            pltpu.VMEM((9, cells_y, cells_z), jnp.float32),
            pltpu.SemaphoreType.DMA((9,)),
        ],
        compiler_params=pltpu.CompilerParams(vmem_limit_bytes=24 * 1024 * 1024),
        cost_estimate=pl.CostEstimate(flops=1_000_000, bytes_accessed=100_000, transcendentals=0),
    )(*operands)


def from_behind(value, axis, steps):
    count = lax.axis_size(axis)
    leading, last = (max(0, -steps), min(count, count - steps))
    return lax.ppermute(value, axis, [(source, source + steps) for source in range(leading, last)])


def around(medium, store, early, count):
    lanes = medium.shape[-1]
    group = lax.axis_index("groups")
    order = [2 * place for place in range((count + 1) // 2)]
    order += [box for box in range(count - 1, 0, -1) if box % 2 == 1]
    up = [(order[place], order[(place + 1) % count]) for place in range(count)]
    down = [(target, source) for source, target in up]

    def across(value):
        return lax.ppermute(value, "groups", [(0, 1), (1, 0)])

    mine = store[0].reshape(-1, lanes)
    other = lax.ppermute(mine, "trial", [(0, 1), (1, 0)])
    lower = lax.axis_index("trial") == 0
    rows = [jnp.where(lower, mine, other), jnp.where(lower, other, mine)]
    filler = jnp.zeros(((-2 * mine.shape[0]) % ROWS, lanes), jnp.float32)
    bricks = [lax.dynamic_index_in_dim(medium, which, 0, False).reshape(-1, lanes) for which in (group, 1 - group)]
    size = bricks[0].shape[0]
    third, half = size // 3, size // 2
    units = size // medium.shape[3]
    first = jnp.concatenate([bricks[0]] + rows + [filler])
    later = bricks[1][:third]
    pieces, parts, row_parts = [[first], [bricks[1]]], [[(0, 0, 0, units, 0)], [(0, 0, 0, units, 0)]], [(0, size, 0)]

    def keep(which, piece, entries):
        parts[which] += [(len(pieces[which]),) + entry for entry in entries]
        pieces[which].append(piece)

    forth, back, forth_later, back_later, rests = first, first, later, later, []
    for distance in range(1, count // 2):
        if distance == 2:
            forth, _ = lax.optimization_barrier((forth, (forth_later, back_later)))
        if distance == 3:
            forth, early = lax.optimization_barrier((forth, early))
        forth, back = lax.ppermute(forth, "box", up), lax.ppermute(back, "box", down)
        for piece, offset in ((forth, -distance), (back, distance)):
            row_parts.append((len(pieces[0]), size, offset))
            keep(0, piece, [(0, 0, units, offset)])
        skip = 0
        if distance < 3:
            skip = third
            forth_later = lax.ppermute(forth_later, "box", up)
            back_later = lax.ppermute(back_later, "box", down)
            for piece, offset in ((forth_later, -distance), (back_later, distance)):
                keep(1, piece, [(0, 0, units // 3, offset)])
        rest = jnp.concatenate([forth[skip:size], back[skip:size]])
        if distance == 3:
            rest, _ = lax.optimization_barrier((rest, rests[1]))
        rest = across(rest)
        rests.append(rest)
        left = units - skip * units // size
        keep(1, rest, [(0, units - left, left, -distance), (size - skip, units - left, left, distance)])
    far = count // 2
    forth, back, _ = lax.optimization_barrier((forth, back, (rests[0], forth_later, back_later)))
    forth, back = lax.ppermute(forth[:half], "box", up), lax.ppermute(back[half:], "box", down)
    row_parts.append((len(pieces[0]) + 1, size - half, far))
    keep(0, forth, [(0, 0, units // 2, far)])
    keep(0, back, [(0, units // 2, units - units // 2, far)])
    rest = across(jnp.concatenate([forth, back[: size - half]]))
    keep(1, rest, [(0, 0, units, far)])
    return ((pieces[0], parts[0], row_parts), (pieces[1], parts[1], [])), early


def hot_planes(offsets, cells_y, cells_z):
    rows = jnp.arange(cells_y, dtype=jnp.int32).reshape(ROWS, cells_y // ROWS).T.reshape(1, cells_y, 1)
    columns = jnp.arange(cells_z, dtype=jnp.int32)[None, None, :]
    hot_y = (offsets[:, None, :] // cells_z == rows).astype(jnp.float32)
    hot_z = (offsets[:, :, None] % cells_z == columns).astype(jnp.bfloat16)
    return hot_y, hot_z


def per_device(medium, store, surf_off, owners, brick_map):
    boxes = lax.axis_size("box")
    place = lax.axis_index("box")
    trials_here, _, all_planes, brick_y, cells_z = medium.shape
    cells_y = boxes * brick_y
    per = surf_off.shape[0] // all_planes
    offsets = surf_off.reshape(all_planes, per)
    reach = STEPS
    pairs = lax.axis_size("trial") == 2 and lax.axis_size("groups") == 2 and trials_here == 2
    if pairs and boxes == 8 and all_planes == 8:
        ring, planes, given = boxes, all_planes, None
        group = lax.axis_index("groups")
        hots = hot_planes(jnp.tile(offsets, (1, cells_z // per)), cells_y, cells_z)
        scalars = [
            jnp.concatenate([jnp.stack([place, slot]), brick_map, owners]) for slot in (group, 1 - group)
        ]
        found, (hots, scalars) = around(medium, store, (hots, scalars), boxes)
    else:
        inverse = jnp.zeros((boxes,), jnp.int32).at[brick_map].set(jnp.arange(boxes, dtype=jnp.int32))
        moved = lax.all_to_all(medium, "box", split_axis=2, concat_axis=3, tiled=True)
        blocks = moved.reshape(trials_here, 3, 1, boxes, brick_y, cells_z)
        mine = jnp.take(blocks, inverse, axis=3).reshape(trials_here, 3, 1, cells_y, cells_z)
        window = jnp.concatenate(
            [from_behind(mine, "box", -shift) for shift in range(-reach, reach + 1)], axis=2
        )
        ring, planes = 1, 2 * reach + 1
        found = [
            ([window[trial].reshape(-1, cells_z)], [(0, 0, 0, 3 * planes, 0)], []) for trial in range(trials_here)
        ]
        slot = place * lax.axis_size("trial") + lax.axis_index("trial")
        rows = lax.psum(jnp.where((owners == slot)[:, None, None], store, 0.0), ("box", "trial"))
        rows = rows.reshape(STEPS * 3, all_planes, per).transpose(1, 0, 2)
        rows = jnp.pad(rows, ((reach, reach), (0, LINES - STEPS * 3), (0, 0)))
        rows = lax.dynamic_slice_in_dim(rows, place, planes, 0)
        given = jnp.tile(rows, (1, 1, cells_z // per))
        offsets = jnp.pad(offsets, ((reach, reach), (0, 0)), constant_values=-1)
        offsets = lax.dynamic_slice_in_dim(offsets, place, planes, 0)
        hots = hot_planes(jnp.tile(offsets, (1, cells_z // per)), cells_y, cells_z)
        scalars = [jnp.stack([place, jnp.int32(trial)]) for trial in range(trials_here)]
    shape = (planes, cells_y, cells_z, per)
    before = None
    for trial in range(trials_here):
        results = run_trial(trials_here, shape, ring, scalars[trial], found[trial], hots, given, before)
        before = results[:2]
        if trial == 0:
            given = results[2]
    return tuple(before)


def solution(mesh):
    return jax.shard_map(
        per_device,
        mesh=mesh,
        in_specs=(
            P("trial", None, None, "box", None),
            P(("groups", "box", "trial"), None, None),
            P(),
            P(),
            P(),
        ),
        out_specs=(
            P(("groups", "trial"), None, "box", None, None),
            P(("groups", "trial"), None, "box", None, None),
        ),
        check_vma=False,
    )
```

```python
import functools

import jax
import jax.numpy as jnp
from jax import lax
from jax.experimental import pallas as pl
from jax.experimental.pallas import tpu as pltpu
from jax.sharding import PartitionSpec as P

STEPS = 6
TIME_STEP = 0.25
VX, VY, VZ, XX, YY, ZZ, XY, XZ, YZ = range(9)
ROWS = 8
LINES = 24
GROUP = 4


def ring_place(box, count):
    return jnp.where(box % 2 == 0, box // 2, count - 1 - box // 2)


def ring_box(place, count):
    return jnp.where(place < count // 2, 2 * place, 2 * (count - 1 - place) + 1)


def ring_offsets(count):
    steps = [0]
    for distance in range(1, count // 2):
        steps += [-distance, distance]
    return steps + [count // 2]


def split_values(value, per):
    group = lax.broadcasted_iota(jnp.int32, value.shape, 1) // per
    high = value.astype(jnp.bfloat16).astype(jnp.float32)
    rest = value - high
    middle = rest.astype(jnp.bfloat16).astype(jnp.float32)
    low = rest - middle
    return jnp.where(
        group == 0, high, jnp.where(group == 1, middle, jnp.where(group == 2, low, 0.0))
    )


class Plane:
    def __init__(self, sources, cells_y, cells_z):
        self.sources, self.chunks = sources, cells_y // ROWS
        row = lax.broadcasted_iota(jnp.int32, (ROWS, cells_z), 0)
        lane = lax.broadcasted_iota(jnp.int32, (ROWS, cells_z), 1)
        self.first_row, self.last_row = row == 0, row == ROWS - 1
        self.first_lane, self.last_lane = lane == 0, lane == cells_z - 1
        self.cells_z = cells_z
        self.loaded, self.rolled = {}, {}

    def fetch(self, chunk):
        if chunk < self.chunks:
            for name, (array, lead) in self.sources.items():
                self.loaded[name, chunk] = array[lead + (slice(chunk * ROWS, chunk * ROWS + ROWS),)]

    def at(self, name, chunk, beside=0):
        return self.loaded[(name, beside) if beside else name, chunk]

    def put(self, name, chunk, value):
        array, lead = self.sources[name]
        array[lead + (slice(chunk * ROWS, chunk * ROWS + ROWS),)] = value

    def roll_rows(self, field, chunk, by):
        if not 0 <= chunk < self.chunks:
            return 0.0
        if (field, chunk) not in self.rolled:
            self.rolled[field, chunk] = pltpu.roll(self.at(field, chunk), by, 0)
        return self.rolled[field, chunk]

    def back_y(self, field, chunk):
        here = self.roll_rows(field, chunk, 1)
        before = self.roll_rows(field, chunk - 1, 1)
        return self.at(field, chunk) - jnp.where(self.first_row, before, here)

    def fore_y(self, field, chunk):
        here = self.roll_rows(field, chunk, ROWS - 1)
        after = self.roll_rows(field, chunk + 1, ROWS - 1)
        return jnp.where(self.last_row, after, here) - self.at(field, chunk)

    def back_x(self, field, chunk):
        return self.at(field, chunk) - self.at(field, chunk, -1)

    def fore_x(self, field, chunk):
        return self.at(field, chunk, 1) - self.at(field, chunk)

    def back_z(self, field, chunk):
        value = self.at(field, chunk)
        return value - jnp.where(self.first_lane, 0.0, pltpu.roll(value, 1, 1))

    def fore_z(self, field, chunk):
        value = self.at(field, chunk)
        return jnp.where(self.last_lane, 0.0, pltpu.roll(value, self.cells_z - 1, 1)) - value


def propagate(plan, *refs):
    parts, row_parts, ring, planes, cells_y, cells_z, per, first = plan
    refs = list(refs)
    scalars = refs[0]
    operands = 1 + max(part[0] for part in parts)
    piece_refs = refs[1 : 1 + operands]
    rest = refs[1 + operands :]
    hot_y, hot_z = rest[:2]
    rest = rest[2:]
    if ring == 1 or not first:
        given_ref = rest[0]
        rest = rest[1:]
    if not first:
        rest = rest[2:]
    vel_ref, str_ref = rest[:2]
    rest = rest[2:]
    if first:
        values = rest[0]
        rest = rest[1:]
    else:
        values = given_ref
    fields, (medium, added, stored, lines, sems) = rest[:9], rest[9:]
    block_y = cells_y // ring
    chunks = cells_y // ROWS

    if ring > 1:
        centre = scalars[0]
        start = ring_place(centre, ring)
        boxes = {
            step: ring_box(lax.rem(start + step + ring, ring), ring) for step in ring_offsets(ring)
        }
        blocks = {step: scalars[2 + box] for step, box in boxes.items()}
    else:
        centre = planes // 2
        blocks = {0: 0}
    for operand, row, first_unit, units, offset in parts:
        top = pl.multiple_of(blocks[offset] * block_y, 8)
        for unit in range(units):
            component, plane = divmod(first_unit + unit, planes)
            source = row + unit * block_y
            medium[component, plane, pl.ds(top, block_y), :] = (
                TIME_STEP * piece_refs[operand][source : source + block_y, :]
            )

    outside = jnp.zeros((cells_y, cells_z), jnp.float32)
    for field in (XY, XZ, VX):
        fields[field][0] = outside
    for field in (XX, VY, VZ):
        fields[field][planes + 1] = outside

    if first and ring > 1:
        halves = planes * per // cells_z
        for operand, row, offset in row_parts:
            stored[boxes[offset]] = piece_refs[operand][row : row + 2 * ROWS, :]
        for step in range(STEPS):
            owner = scalars[2 + ring + step]
            for comp in range(3):
                for half in range(halves):
                    source = (owner % 2) * 3 * halves + comp * halves + half
                    lines[half, pl.ds(step * 3 + comp, 1), :] = stored[owner // 2, pl.ds(source, 1), :]
        for plane in range(planes):
            half, begin = divmod(plane * per, cells_z)
            line = lines[half]
            group = lax.broadcasted_iota(jnp.int32, line.shape, 1) // per
            spread = pltpu.roll(line, cells_z - begin, 1) if begin else line
            spread = jnp.where(
                group == 0,
                spread,
                jnp.where(group == 1, pltpu.roll(spread, per, 1), pltpu.roll(spread, 2 * per, 1)),
            )
            values[plane] = split_values(spread, per)
    elif first:
        for plane in range(planes):
            values[plane] = split_values(given_ref[plane], per)

    def inject(step, plane, begin, size):
        spots = hot_y[plane, begin : begin + size]
        rows = [values[plane, pl.ds(step * 3 + comp, 1), :] for comp in range(3)]
        weighted = jnp.concatenate([(spots * row).astype(jnp.bfloat16) for row in rows], axis=0)
        found = jnp.dot(weighted, hot_z[plane], preferred_element_type=jnp.float32)
        return [found[comp * size : comp * size + size] for comp in range(3)]

    def limits(step):
        reach = STEPS - 1 - step
        return jnp.maximum(centre - reach, 0), jnp.minimum(centre + reach, planes - 1)

    def beside(field, index, step=0):
        return fields[field], (index + step,)

    def velocity(components, plane, carry):
        index = plane + 1
        sources = {"gain": (medium, (2, plane))}
        for field in components:
            sources[field] = beside(field, index)
            sources["added", field] = (added, (field, plane))
        if VX in components:
            sources.update({XX: beside(XX, index), (XX, 1): beside(XX, index, 1)})
        if VY in components:
            sources.update({(XY, -1): beside(XY, index, -1), YY: beside(YY, index)})
        if VZ in components:
            sources.update({(XZ, -1): beside(XZ, index, -1), ZZ: beside(ZZ, index)})
        if VY in components or VZ in components:
            sources[YZ] = beside(YZ, index)
        sources.update({XY: beside(XY, index), XZ: beside(XZ, index)})
        here = Plane(sources, cells_y, cells_z)
        here.fetch(0)
        for chunk in range(chunks):
            here.fetch(chunk + 1)
            gain = here.at("gain", chunk)
            pulls = []
            if VX in components:
                pull = here.fore_x(XX, chunk) + here.back_y(XY, chunk) + here.back_z(XZ, chunk)
                pulls.append((VX, pull))
            if VY in components:
                pull = here.back_x(XY, chunk) + here.fore_y(YY, chunk) + here.back_z(YZ, chunk)
                pulls.append((VY, pull))
            if VZ in components:
                pull = here.back_x(XZ, chunk) + here.back_y(YZ, chunk) + here.fore_z(ZZ, chunk)
                pulls.append((VZ, pull))
            news = [
                (comp, here.at(comp, chunk) + gain * pull + here.at(("added", comp), chunk))
                for comp, pull in pulls
            ]
            for comp, new in news:
                here.put(comp, chunk, new)
        return carry

    def stress(step, fresh, final, plane, carry):
        index = plane + 1
        sources = {"lam": (medium, (0, plane)), "mu": (medium, (1, plane))}
        sources.update({field: beside(field, index) for field in range(3 if fresh else 9)})
        sources.update({(field, by): beside(field, index, by) for field, by in ((VX, -1), (VY, 1), (VZ, 1))})
        if fresh:
            targets = Plane({field: beside(field, index) for field in range(3, 9)}, cells_y, cells_z)
        here = Plane(sources, cells_y, cells_z)
        here.fetch(0)
        for chunk in range(chunks):
            if not final and chunk % GROUP == 0:
                begin = chunk * ROWS
                found = inject(step + 1, plane, begin, GROUP * ROWS)
            here.fetch(chunk + 1)
            lam, mu = here.at("lam", chunk), here.at("mu", chunk)
            twice = mu + mu
            grad_x, grad_y, grad_z = here.back_x(VX, chunk), here.back_y(VY, chunk), here.back_z(VZ, chunk)
            spread = lam * (grad_x + grad_y + grad_z)
            changes = (
                (XX, spread + twice * grad_x),
                (YY, spread + twice * grad_y),
                (ZZ, spread + twice * grad_z),
                (XY, mu * (here.fore_y(VX, chunk) + here.fore_x(VY, chunk))),
                (XZ, mu * (here.fore_z(VX, chunk) + here.fore_x(VZ, chunk))),
                (YZ, mu * (here.fore_z(VY, chunk) + here.fore_y(VZ, chunk))),
            )
            if fresh:
                for field, change in changes:
                    targets.put(field, chunk, change)
            else:
                news = [(field, here.at(field, chunk) + change) for field, change in changes]
                for field, new in news:
                    here.put(field, chunk, new)
            if not final and chunk % GROUP == GROUP - 1:
                for comp, value in enumerate(found):
                    added[comp, plane, begin : begin + GROUP * ROWS] = value
        return carry

    def velocities(step):
        low, high = limits(step)
        lax.fori_loop(jnp.maximum(low - 1, 0), low, functools.partial(velocity, (VX,)), 0)
        lax.fori_loop(low, high + 1, functools.partial(velocity, (VX, VY, VZ)), 0)
        lax.fori_loop(high + 1, jnp.minimum(high + 2, planes), functools.partial(velocity, (VY, VZ)), 0)

    for plane in range(planes):
        for comp, value in enumerate(inject(0, plane, 0, cells_y)):
            fields[comp][plane + 1] = value
    low, high = limits(0)
    lax.fori_loop(low, high + 1, functools.partial(stress, 0, True, False), 0)

    def one_step(step, carry):
        velocities(step)
        low, high = limits(step)
        lax.fori_loop(low, high + 1, functools.partial(stress, step, False, False), 0)
        return carry

    lax.fori_loop(1, STEPS - 1, one_step, 0)
    trial = scalars[1]
    copies = []
    for field in range(9):
        target = vel_ref.at[trial, field, 0] if field < 3 else str_ref.at[trial, field - 3, 0]
        copies.append(pltpu.make_async_copy(fields[field].at[centre + 1], target, sems.at[field]))
    velocities(STEPS - 1)
    for copy in copies[:3]:
        copy.start()
    stress(STEPS - 1, False, True, centre, 0)
    for copy in copies[3:]:
        copy.start()
    for copy in copies:
        copy.wait()


def run_trial(trials, shape, ring, scalars, found, hots, given, before):
    planes, cells_y, cells_z, per = shape
    pieces, parts, row_parts = found
    first = before is None
    smem, vmem, anywhere = (
        pl.BlockSpec(memory_space=space) for space in (pltpu.SMEM, pltpu.VMEM, pl.ANY)
    )
    operands = [scalars] + list(pieces) + list(hots)
    specs = [smem] + [vmem] * (len(operands) - 1)
    if given is not None:
        operands.append(given)
        specs.append(vmem)
    out_shape = [
        jax.ShapeDtypeStruct((trials, 3, 1, cells_y, cells_z), jnp.float32),
        jax.ShapeDtypeStruct((trials, 6, 1, cells_y, cells_z), jnp.float32),
    ]
    out_specs = [anywhere, anywhere]
    aliases = {}
    if first:
        out_shape.append(jax.ShapeDtypeStruct((planes, LINES, cells_z), jnp.float32))
        out_specs.append(vmem)
    else:
        aliases = {len(operands): 0, len(operands) + 1: 1}
        operands += list(before)
        specs += [anywhere, anywhere]
    field = pltpu.VMEM((planes + 2, cells_y, cells_z), jnp.float32)
    return pl.pallas_call(
        functools.partial(propagate, (parts, row_parts, ring, planes, cells_y, cells_z, per, first)),
        out_shape=out_shape,
        in_specs=specs,
        out_specs=out_specs,
        input_output_aliases=aliases,
        scratch_shapes=[field] * 9
        + [
            pltpu.VMEM((3, planes, cells_y, cells_z), jnp.float32),
            pltpu.VMEM((3, planes, cells_y, cells_z), jnp.float32),
            pltpu.VMEM((ring, 2 * ROWS, cells_z), jnp.float32),
            pltpu.VMEM((2, LINES, cells_z), jnp.float32),
            pltpu.SemaphoreType.DMA((9,)),
        ],
        compiler_params=pltpu.CompilerParams(vmem_limit_bytes=40 * 1024 * 1024),
        cost_estimate=pl.CostEstimate(flops=30_000_000, bytes_accessed=5_000_000, transcendentals=0),
    )(*operands)


def from_behind(value, axis, steps):
    count = lax.axis_size(axis)
    leading, last = (max(0, -steps), min(count, count - steps))
    return lax.ppermute(value, axis, [(source, source + steps) for source in range(leading, last)])


def around(medium, store, count):
    lanes = medium.shape[-1]
    group = lax.axis_index("groups")
    order = [2 * place for place in range((count + 1) // 2)]
    order += [box for box in range(count - 1, 0, -1) if box % 2 == 1]
    up = [(order[place], order[(place + 1) % count]) for place in range(count)]
    down = [(target, source) for source, target in up]

    def across(value):
        return lax.ppermute(value, "groups", [(0, 1), (1, 0)])

    mine = store[0].reshape(-1, lanes)
    other = lax.ppermute(mine, "trial", [(0, 1), (1, 0)])
    lower = lax.axis_index("trial") == 0
    rows = [jnp.where(lower, mine, other), jnp.where(lower, other, mine)]
    filler = jnp.zeros(((-2 * mine.shape[0]) % ROWS, lanes), jnp.float32)
    bricks = [lax.dynamic_index_in_dim(medium, which, 0, False).reshape(-1, lanes) for which in (group, 1 - group)]
    size = bricks[0].shape[0]
    third, half = size // 3, size // 2
    units = size // medium.shape[3]
    first = jnp.concatenate([bricks[0]] + rows + [filler])
    later = bricks[1][:third]
    pieces, parts, row_parts = [[first], [bricks[1]]], [[(0, 0, 0, units, 0)], [(0, 0, 0, units, 0)]], [(0, size, 0)]

    def keep(which, piece, entries):
        parts[which] += [(len(pieces[which]),) + entry for entry in entries]
        pieces[which].append(piece)

    forth, back, forth_later, back_later, rests = first, first, later, later, []
    for distance in range(1, count // 2):
        forth, back = lax.ppermute(forth, "box", up), lax.ppermute(back, "box", down)
        forth_later = lax.ppermute(forth_later, "box", up)
        back_later = lax.ppermute(back_later, "box", down)
        rest = across(jnp.concatenate([forth[third:size], back[third:size]]))
        rests.append(rest)
        for piece, offset in ((forth, -distance), (back, distance)):
            row_parts.append((len(pieces[0]), size, offset))
            keep(0, piece, [(0, 0, units, offset)])
        for piece, offset in ((forth_later, -distance), (back_later, distance)):
            keep(1, piece, [(0, 0, units // 3, offset)])
        left = units - units // 3
        keep(1, rest, [(0, units - left, left, -distance), (size - third, units - left, left, distance)])
    far = count // 2
    forth, back, _ = lax.optimization_barrier((forth, back, rests[0]))
    forth, back = lax.ppermute(forth[:half], "box", up), lax.ppermute(back[half:], "box", down)
    row_parts.append((len(pieces[0]) + 1, size - half, far))
    keep(0, forth, [(0, 0, units // 2, far)])
    keep(0, back, [(0, units // 2, units - units // 2, far)])
    keep(1, lax.ppermute(forth_later, "box", up), [(0, 0, units // 3, far)])
    rest = across(jnp.concatenate([forth[third:], back[: size - half]]))
    pieces[0][-1], _ = lax.optimization_barrier((pieces[0][-1], rests[1]))
    keep(1, rest, [(0, units // 3, units - units // 3, far)])
    return ((pieces[0], parts[0], row_parts), (pieces[1], parts[1], []))


def hot_planes(offsets, cells_y, cells_z):
    rows = jnp.arange(cells_y, dtype=jnp.int32)[None, :, None]
    columns = jnp.arange(cells_z, dtype=jnp.int32)[None, None, :]
    hot_y = (offsets[:, None, :] // cells_z == rows).astype(jnp.float32)
    hot_z = (offsets[:, :, None] % cells_z == columns).astype(jnp.bfloat16)
    return hot_y, hot_z


def per_device(medium, store, surf_off, owners, brick_map):
    boxes = lax.axis_size("box")
    place = lax.axis_index("box")
    trials_here, _, all_planes, brick_y, cells_z = medium.shape
    cells_y = boxes * brick_y
    per = surf_off.shape[0] // all_planes
    offsets = surf_off.reshape(all_planes, per)
    reach = STEPS
    pairs = lax.axis_size("trial") == 2 and lax.axis_size("groups") == 2 and trials_here == 2
    if pairs and boxes == 8 and all_planes == 8:
        ring, planes, given = boxes, all_planes, None
        group = lax.axis_index("groups")
        hots = hot_planes(jnp.tile(offsets, (1, cells_z // per)), cells_y, cells_z)
        scalars = [
            jnp.concatenate([jnp.stack([place, slot]), brick_map, owners]) for slot in (group, 1 - group)
        ]
        found = around(medium, store, boxes)
    else:
        inverse = jnp.zeros((boxes,), jnp.int32).at[brick_map].set(jnp.arange(boxes, dtype=jnp.int32))
        moved = lax.all_to_all(medium, "box", split_axis=2, concat_axis=3, tiled=True)
        blocks = moved.reshape(trials_here, 3, 1, boxes, brick_y, cells_z)
        mine = jnp.take(blocks, inverse, axis=3).reshape(trials_here, 3, 1, cells_y, cells_z)
        window = jnp.concatenate(
            [from_behind(mine, "box", -shift) for shift in range(-reach, reach + 1)], axis=2
        )
        ring, planes = 1, 2 * reach + 1
        found = [
            ([window[trial].reshape(-1, cells_z)], [(0, 0, 0, 3 * planes, 0)], []) for trial in range(trials_here)
        ]
        slot = place * lax.axis_size("trial") + lax.axis_index("trial")
        rows = lax.psum(jnp.where((owners == slot)[:, None, None], store, 0.0), ("box", "trial"))
        rows = rows.reshape(STEPS * 3, all_planes, per).transpose(1, 0, 2)
        rows = jnp.pad(rows, ((reach, reach), (0, LINES - STEPS * 3), (0, 0)))
        rows = lax.dynamic_slice_in_dim(rows, place, planes, 0)
        given = jnp.tile(rows, (1, 1, cells_z // per))
        offsets = jnp.pad(offsets, ((reach, reach), (0, 0)), constant_values=-1)
        offsets = lax.dynamic_slice_in_dim(offsets, place, planes, 0)
        hots = hot_planes(jnp.tile(offsets, (1, cells_z // per)), cells_y, cells_z)
        scalars = [jnp.stack([place, jnp.int32(trial)]) for trial in range(trials_here)]
    shape = (planes, cells_y, cells_z, per)
    before = None
    for trial in range(trials_here):
        results = run_trial(trials_here, shape, ring, scalars[trial], found[trial], hots, given, before)
        before = results[:2]
        if trial == 0:
            given = results[2]
    return tuple(before)


def solution(mesh):
    return jax.shard_map(
        per_device,
        mesh=mesh,
        in_specs=(
            P("trial", None, None, "box", None),
            P(("groups", "box", "trial"), None, None),
            P(),
            P(),
            P(),
        ),
        out_specs=(
            P(("groups", "trial"), None, "box", None, None),
            P(("groups", "trial"), None, "box", None, None),
        ),
        check_vma=False,
    )
```
